32 devices in a mesh: seq: 16 (over z, y, core), head: 2 (over x).
Axes of the slice: x: 2, y: 2, z: 4, core: 2. Of those that a mesh axis runs over, the one named last changes fastest.
Arguments:
- queries: bfloat16 [8192, 4096], P(('seq', 'head')), may hold values from -25 to 25
- key_rows: bfloat16 [8192, 4096], P(('seq', 'head')), may hold values from -6 to 6
- value_rows: bfloat16 [8192, 4096], P(('seq', 'head')), may hold values from -6 to 6
- out_grad: bfloat16 [8192, 4096], P(('seq', 'head')), may hold values from -6 to 6
- doc_ids: int32 [8192], replicated, may hold values from 0 to 3, never falling along the last dimension, each value on 1 to 4096 neighbouring positions
- picks: int32 [16, 32, 2], P('seq', 'head'), may hold values from 1 to 3, as said below
Outputs:
- attn_out: bfloat16 [8192, 4096], P(('seq', 'head'))
- query_grad: bfloat16 [8192, 4096], P(('seq', 'head'))
- key_grad: bfloat16 [8192, 4096], P(('seq', 'head'))
- value_grad: bfloat16 [8192, 4096], P(('seq', 'head'))
The draws below stay inside these ranges and needn't reach their ends.
Inputs may be any that keep to these rules, and one draw needn't show every extreme that they name: `doc_ids`: never falling along the tokens; each document is at most 4096 tokens, one exactly that long. `picks`: for each block and head, 2 different offsets.
All inputs are finite; a program needn't handle non-finite values.
Results may differ from the reference program's by a relative error of at most 0.027.
Values may be sent and summed in bfloat16 or wider, within the bound.
A program may use at most 128 MiB of HBM per device.

```python
import math
import jax
import jax.numpy as jnp
import numpy as np
from jax import lax

HEADS = 32
HEAD_DIM = 128
D = 4096
BLOCK = 512
TOPK = 2
REACH = 3
TOK_DEV = 512
TOKENS = 8192
NBLK = 16
DOCS = 4
N_SEQ = 16


def draw_queries(key, part):
    key = jax.random.fold_in(key, 1)
    return jnp.clip(jax.random.normal(key, (TOKENS, D), jnp.float32), -6.0, 6.0).astype(jnp.bfloat16)


def draw_key_rows(key, part):
    key = jax.random.fold_in(key, 2)
    return jnp.clip(jax.random.normal(key, (TOKENS, D), jnp.float32), -6.0, 6.0).astype(jnp.bfloat16)


def draw_picks(key, part):
    key = jax.random.fold_in(key, 3)
    raw = jax.random.randint(key, (NBLK, HEADS, REACH), 0, 1048576)
    ranked = raw * REACH + jnp.arange(REACH, dtype=jnp.int32)
    order = jnp.argsort(ranked, axis=-1)
    return (order[..., :TOPK] + 1).astype(jnp.int32)


def block_levels(stream_key, shape, shards, smallest, largest):
    gain = 1.0
    for position, parts in shards:
        steps = jax.random.uniform(jax.random.fold_in(jax.random.fold_in(stream_key, 6), position), (parts,), jnp.float32, smallest / len(shards), largest / len(shards))
        gain = gain * jnp.repeat(jnp.exp(steps), shape[position] // parts).reshape((-1,) + (1,) * (len(shape) - 1 - position))
    return gain


def length_profile(number_of, total, limit, lean):
    loads = [(1 << 20) // math.isqrt(grade ** lean) + 1 for grade in range(2, number_of + 1)]
    rest, counts = total - limit - (number_of - 1), [1] * (number_of - 1)
    while rest > 0:
        candidates = [i for i in range(number_of - 1) if counts[i] < limit]
        mass, budget = sum([loads[i] for i in candidates]), rest
        for i in candidates:
            addition = min(limit - counts[i], max(1, budget * loads[i] // mass), rest)
            counts[i] = counts[i] + addition
            rest = rest - addition
    return np.array([limit] + counts)


def ragged_sizes(stream_key, number_of, total, most, skew):
    if number_of == 2:
        one = jax.random.randint(stream_key, (), max(1, total - most), min(most, total - 1) + 1)
        return jnp.stack([one, total - one])
    lengths = jnp.asarray(length_profile(number_of, total, most, skew), jnp.int32)
    couples = (number_of - 1) // 2
    giver, sink = lengths[1:1 + 2 * couples:2], lengths[2:2 + 2 * couples:2]
    slack = jnp.minimum(giver - 1, most - sink)
    moved = jax.random.randint(jax.random.fold_in(stream_key, 1), (couples,), 0, 1 << 20) % (slack + 1)
    lengths = lengths.at[1:1 + 2 * couples:2].set(giver - moved).at[2:2 + 2 * couples:2].set(sink + moved)
    return lengths[jax.random.permutation(jax.random.fold_in(stream_key, 2), number_of)]


def normal_values(own_key, extent, width, bound, shards=(), held_as=jnp.bfloat16):
    values = jax.random.normal(own_key, extent, jnp.float32) * width
    if len(shards) > 0:
        values = block_levels(own_key, extent, shards, -0.22, 0.18) * values
    return jnp.clip(values, min=-bound, max=bound).astype(held_as)


def setup_inputs(seed: int = 0) -> dict:
    arg_keys = jax.random.split(jax.random.key(seed), 7)
    return {
        "queries": draw_queries(jax.random.fold_in(arg_keys[6], 71), 0),
        "key_rows": draw_key_rows(jax.random.fold_in(arg_keys[6], 71), 0),
        "value_rows": normal_values(arg_keys[2], (TOKENS, D), 1.0, 6.0, ((0, 32),)),
        "out_grad": normal_values(arg_keys[3], (TOKENS, D), 1.0, 6.0, ((0, 32),)),
        "doc_ids": jnp.searchsorted(jnp.cumsum(ragged_sizes(arg_keys[4], DOCS, TOKENS, 8 * BLOCK, 0)), jnp.arange(TOKENS), side="right").astype(jnp.int32),
        "picks": draw_picks(jax.random.fold_in(arg_keys[6], 71), 0),
    }


NEGATIVE = -1.0e30


def block_masks(picks_block, own_index, docs_query, docs_window):
    head_count = picks_block.shape[0]
    slot_count = docs_window.shape[0]
    block_rows = docs_query.shape[0]
    chosen = jnp.concatenate([own_index - picks_block, jnp.full((head_count, 1), own_index, jnp.int32)], axis=1).astype(jnp.int32)
    onehot = chosen[:, :, None] == jnp.arange(slot_count, dtype=jnp.int32)[None, None, :]
    docs_chosen = docs_window[chosen]
    key_count = chosen.shape[1]
    causal = jnp.arange(block_rows)[None, :] <= jnp.arange(block_rows)[:, None]
    earlier = jnp.arange(key_count) < key_count - 1
    allowed = jnp.logical_or(earlier[None, :, None], causal[:, None, :])
    same_doc = docs_query[None, :, None, None] == docs_chosen[:, None, :, :]
    return onehot, jnp.logical_and(same_doc, allowed[None])


def choose_rows(onehot, window):
    return jnp.einsum('hkw,wbhe->hkbe', onehot.astype(jnp.float32), window.astype(jnp.float32))


def masked_scores(query_head, keys_head, mask_head, score_scale):
    scores = jnp.einsum('be,kce->bkc', query_head.astype(jnp.float32), keys_head.astype(jnp.float32)) * score_scale
    return jnp.where(mask_head, scores, NEGATIVE)


def forward_heads(query_block, keys_chosen, values_chosen, allowed_mask, score_scale):
    def one_head(pieces):
        query_head, keys_head, values_head, mask_head = pieces
        scores = masked_scores(query_head, keys_head, mask_head, score_scale)
        row_max = jnp.max(scores, axis=(1, 2), keepdims=True)
        row_total = jnp.sum(jnp.exp(scores - row_max), axis=(1, 2), keepdims=True)
        log_total = row_max + jnp.log(row_total)
        probs_low = jnp.exp(scores - log_total).astype(jnp.bfloat16)
        result = jnp.einsum('bkc,kce->be', probs_low.astype(jnp.float32), values_head.astype(jnp.float32)).astype(jnp.bfloat16)
        return result, log_total[:, 0, 0]

    results, logs = lax.map(one_head, (jnp.swapaxes(query_block, 0, 1), keys_chosen, values_chosen, allowed_mask))
    return jnp.swapaxes(results, 0, 1), logs


def backward_heads(query_block, grad_block, out_block, log_block, keys_chosen, values_chosen, allowed_mask, onehot, score_scale):
    def one_head(pieces):
        query_head, grad_head, out_head, log_head, keys_head, values_head, mask_head, place_head = pieces
        scores = masked_scores(query_head, keys_head, mask_head, score_scale)
        probs_full = jnp.exp(scores - log_head[:, None, None])
        probs_low = probs_full.astype(jnp.bfloat16)
        delta = jnp.sum(grad_head.astype(jnp.float32) * out_head.astype(jnp.float32), axis=1)
        prob_grad = jnp.einsum('be,kce->bkc', grad_head.astype(jnp.float32), values_head.astype(jnp.float32))
        score_grad = (probs_full * (prob_grad - delta[:, None, None]) * score_scale).astype(jnp.bfloat16)
        query_part = jnp.einsum('bkc,kce->be', score_grad.astype(jnp.float32), keys_head.astype(jnp.float32))
        key_part = jnp.einsum('bkc,be->kce', score_grad.astype(jnp.float32), query_head.astype(jnp.float32))
        value_part = jnp.einsum('bkc,be->kce', probs_low.astype(jnp.float32), grad_head.astype(jnp.float32))
        placing = place_head.astype(jnp.float32)
        key_slots = jnp.einsum('kw,kce->wce', placing, key_part, precision=lax.Precision.HIGHEST)
        value_slots = jnp.einsum('kw,kce->wce', placing, value_part, precision=lax.Precision.HIGHEST)
        return query_part, key_slots, value_slots

    query_parts, key_slots, value_slots = lax.map(one_head, (jnp.swapaxes(query_block, 0, 1), jnp.swapaxes(grad_block, 0, 1), jnp.swapaxes(out_block, 0, 1), log_block, keys_chosen, values_chosen, allowed_mask, onehot))
    return jnp.swapaxes(query_parts, 0, 1), jnp.transpose(key_slots, (1, 2, 0, 3)), jnp.transpose(value_slots, (1, 2, 0, 3))


def reference(queries, key_rows, value_rows, out_grad, doc_ids, picks):
    block_count = TOK_DEV // BLOCK
    shifts = (REACH + block_count - 1) // block_count
    slot_count = (shifts + 1) * block_count
    feature_width = HEADS * HEAD_DIM
    pad_rows = shifts * TOK_DEV
    score_scale = HEAD_DIM ** -0.5

    def padded(array):
        zeros = jnp.zeros((pad_rows, feature_width), array.dtype)
        return jnp.concatenate([zeros, array], axis=0).reshape(-1, BLOCK, HEADS, HEAD_DIM)

    keys_pad = padded(key_rows)
    values_pad = padded(value_rows)
    docs_pad = jnp.concatenate([jnp.full((pad_rows,), -1, jnp.int32), doc_ids.astype(jnp.int32)])
    query_dev = queries.reshape(N_SEQ, block_count, BLOCK, HEADS, HEAD_DIM)
    grad_dev = out_grad.reshape(N_SEQ, block_count, BLOCK, HEADS, HEAD_DIM)
    picks_dev = picks.reshape(N_SEQ, block_count, HEADS, TOPK)

    def device_step(totals, pieces):
        key_acc, value_acc = totals
        seq_index, query_here, grad_here, picks_here = pieces
        first_block = (seq_index * block_count).astype(jnp.int32)
        key_window = lax.dynamic_slice_in_dim(keys_pad, first_block, slot_count, 0)
        value_window = lax.dynamic_slice_in_dim(values_pad, first_block, slot_count, 0)
        docs_window = lax.dynamic_slice_in_dim(docs_pad, (seq_index * TOK_DEV).astype(jnp.int32), slot_count * BLOCK, 0).reshape(slot_count, BLOCK)
        key_sum = jnp.zeros((slot_count, BLOCK, HEADS, HEAD_DIM), jnp.float32)
        value_sum = jnp.zeros((slot_count, BLOCK, HEADS, HEAD_DIM), jnp.float32)
        out_blocks = []
        query_blocks = []
        for local in range(block_count):
            own_index = shifts * block_count + local
            onehot, allowed_mask = block_masks(picks_here[local], own_index, docs_window[own_index], docs_window)
            keys_chosen = choose_rows(onehot, key_window)
            values_chosen = choose_rows(onehot, value_window)
            out_block, log_block = forward_heads(query_here[local], keys_chosen, values_chosen, allowed_mask, score_scale)
            query_part, key_slots, value_slots = backward_heads(query_here[local], grad_here[local], out_block, log_block, keys_chosen, values_chosen, allowed_mask, onehot, score_scale)
            key_sum = key_sum + key_slots
            value_sum = value_sum + value_slots
            out_blocks.append(out_block)
            query_blocks.append(query_part.astype(jnp.bfloat16))
        key_low = lax.optimization_barrier(key_sum.astype(jnp.bfloat16)).astype(jnp.float32)
        value_low = lax.optimization_barrier(value_sum.astype(jnp.bfloat16)).astype(jnp.float32)
        key_acc = lax.dynamic_update_slice_in_dim(key_acc, lax.dynamic_slice_in_dim(key_acc, first_block, slot_count, 0) + key_low, first_block, 0)
        value_acc = lax.dynamic_update_slice_in_dim(value_acc, lax.dynamic_slice_in_dim(value_acc, first_block, slot_count, 0) + value_low, first_block, 0)
        return (key_acc, value_acc), (jnp.stack(out_blocks), jnp.stack(query_blocks))

    start_totals = (jnp.zeros(keys_pad.shape, jnp.float32), jnp.zeros(values_pad.shape, jnp.float32))
    (key_acc, value_acc), (outs_all, query_all) = lax.scan(device_step, start_totals, (jnp.arange(N_SEQ, dtype=jnp.int32), query_dev, grad_dev, picks_dev))
    attn_out = outs_all.reshape(TOKENS, feature_width)
    query_grad = query_all.reshape(TOKENS, feature_width)
    key_grad = key_acc[shifts * block_count:].reshape(TOKENS, feature_width).astype(jnp.bfloat16)
    value_grad = value_acc[shifts * block_count:].reshape(TOKENS, feature_width).astype(jnp.bfloat16)
    return attn_out, query_grad, key_grad, value_grad
```

```python
import functools
import jax
import jax.numpy as jnp
from jax import lax
from jax.experimental import pallas as pl
from jax.experimental.pallas import tpu as pltpu
from jax.sharding import PartitionSpec as P

HEAD_DIM = 128
BLOCK = 512
REACH = 3
NEGATIVE = -1e30
CHUNKS = 2


def nt(a, b):
    return lax.dot_general(a, b, (((1,), (1,)), ((), ())), preferred_element_type=jnp.float32)


def nn(a, b):
    return lax.dot_general(a, b, (((1,), (0,)), ((), ())), preferred_element_type=jnp.float32)


def one_head(q, g, keys, values, biases):
    scale = HEAD_DIM**-0.5
    scores = [nt(k, q) * scale + b for k, b in zip(keys, biases)]
    top = functools.reduce(
        jnp.maximum, [jnp.max(s, axis=0, keepdims=True) for s in scores]
    )
    exps = [jnp.exp(s - top) for s in scores]
    total = functools.reduce(jnp.add, [jnp.sum(e, axis=0, keepdims=True) for e in exps])
    inverse = 1.0 / total
    probs = [e * inverse for e in exps]
    lows = [p.astype(jnp.bfloat16) for p in probs]
    out_t = functools.reduce(
        jnp.add, [nn(v.T, p) for v, p in zip(values, lows)]
    )
    out_low = out_t.astype(jnp.bfloat16)
    g_t = g.astype(jnp.float32).T
    delta = jnp.sum(out_low.astype(jnp.float32) * g_t, axis=0, keepdims=True)
    grads = [
        (p * (nt(v, g) - delta)).astype(jnp.bfloat16) for p, v in zip(probs, values)
    ]
    dq_t = functools.reduce(jnp.add, [nn(k.T, d) for k, d in zip(keys, grads)]) * scale
    dks = [nn(d, q) * scale for d in grads]
    dvs = [nn(p, g) for p in lows]
    return out_t.T.astype(jnp.bfloat16), dq_t.T.astype(jnp.bfloat16), dks, dvs


def attend(slots, docs_q, docs_k, qg, own, near, mid, far, out, parts, bias):
    i = pl.program_id(0)

    @pl.when(i == 0)
    def _():
        rows = lax.broadcasted_iota(jnp.int32, (BLOCK, BLOCK), 0)
        cols = lax.broadcasted_iota(jnp.int32, (BLOCK, BLOCK), 1)
        for w in range(4):
            ok = docs_k[w] == docs_q[...]
            if w == 3:
                ok = jnp.logical_and(ok, rows <= cols)
            bias[w] = jnp.where(ok, 0.0, NEGATIVE)

    a, b = slots[0, i], slots[1, i]

    def pick(n, which):
        return jnp.where(n == 0, near[which], jnp.where(n == 1, mid[which], far[which]))

    keys = [pick(a, 0), pick(b, 0), own[0]]
    values = [pick(a, 1), pick(b, 1), own[1]]
    biases = [bias[a], bias[b], bias[3]]
    o, dq, dks, dvs = one_head(qg[0], qg[1], keys, values, biases)
    out[0] = o
    out[1] = dq
    for which, d in ((0, dks), (1, dvs)):
        parts[3, which] = d[2].astype(jnp.bfloat16)
        for w in range(3):
            here = jnp.where(a == w, d[0], jnp.where(b == w, d[1], 0.0))
            parts[w, which] = here.astype(jnp.bfloat16)


def attention(slots, docs_q, docs_k, qg, own, near, mid, far):
    heads = qg.shape[2] // HEAD_DIM
    pair = pl.BlockSpec((2, BLOCK, HEAD_DIM), lambda i, *_: (0, 0, i))
    width = qg.shape[2]
    return pl.pallas_call(
        attend,
        grid_spec=pltpu.PrefetchScalarGridSpec(
            num_scalar_prefetch=1,
            grid=(heads,),
            in_specs=[
                pl.BlockSpec((1, BLOCK), lambda i, *_: (0, 0)),
                pl.BlockSpec((4, BLOCK, 1), lambda i, *_: (0, 0, 0)),
                pair,
                pair,
                pair,
                pair,
                pair,
            ],
            out_specs=[
                pair,
                pl.BlockSpec((4, 2, BLOCK, HEAD_DIM), lambda i, *_: (0, 0, 0, i)),
            ],
            scratch_shapes=[pltpu.VMEM((4, BLOCK, BLOCK), jnp.float32)],
        ),
        out_shape=[
            jax.ShapeDtypeStruct((2, BLOCK, width), jnp.bfloat16),
            jax.ShapeDtypeStruct((4, 2, BLOCK, width), jnp.bfloat16),
        ],
        compiler_params=pltpu.CompilerParams(
            dimension_semantics=("arbitrary",), vmem_limit_bytes=50 * 2**20
        ),
        cost_estimate=pl.CostEstimate(
            flops=heads * 12 * 128 * 512 * 1536 * 3,
            bytes_accessed=20 * BLOCK * width * 2,
            transcendentals=heads * 512 * 1536,
        ),
    )(slots, docs_q, docs_k, qg, own, near, mid, far)


def per_device(queries, key_rows, value_rows, out_grad, doc_ids, picks):
    peers = lax.axis_size("head")
    length = lax.axis_size("seq")
    seq = lax.axis_index("seq")
    rank = lax.axis_index("head")
    rows = queries.shape[0]
    width = queries.shape[1] // peers
    heads = width // HEAD_DIM
    chunks = CHUNKS
    part = width // chunks

    def gather_heads(arrays, c):
        x = jnp.stack(arrays)

        if peers != 2:
            x = x.reshape(2, rows, peers, width)[..., c * part : (c + 1) * part]
            x = lax.all_to_all(x, "head", split_axis=2, concat_axis=1, tiled=True)
            return x.reshape(2, rows * peers, part)

        def columns(r):
            return lax.dynamic_slice_in_dim(x, r * width + c * part, part, 2)

        mine = columns(rank)
        theirs = lax.ppermute(columns(1 - rank), "head", [(0, 1), (1, 0)])
        return jnp.where(
            rank == 0,
            jnp.concatenate([mine, theirs], axis=1),
            jnp.concatenate([theirs, mine], axis=1),
        )

    def give_tokens(x):
        if peers != 2:
            x = lax.all_to_all(x, "head", split_axis=1, concat_axis=2, tiled=True)
            return x.reshape(2, rows, peers, part)

        def tokens(r):
            return lax.dynamic_slice_in_dim(x, r * rows, rows, 1)

        mine = tokens(rank)
        theirs = lax.ppermute(tokens(1 - rank), "head", [(0, 1), (1, 0)])
        return jnp.where(
            rank == 0,
            jnp.stack([mine, theirs], axis=2),
            jnp.stack([theirs, mine], axis=2),
        )

    def inside(pairs):
        return [(a, b) for a, b in pairs if 0 <= a < length and 0 <= b < length]

    two = inside([(s, s + 2) for s in range(length)])
    odd = inside([(s, s + 1 if s % 2 == 0 else s + 3) for s in range(length)])
    mate = inside([(s, s ^ 1) for s in range(length)])

    def back(pairs):
        return [(b, a) for a, b in pairs]

    parity = seq % 2
    local = picks[0].T
    slots = jnp.where(local == 2, 1, jnp.where((local == 1) == (parity == 1), 0, 2))
    offsets = jnp.stack(
        [jnp.where(parity == 1, 1, 3), jnp.int32(2), jnp.where(parity == 1, 3, 1), jnp.int32(0)]
    )
    docs_pad = jnp.concatenate([jnp.full((REACH * BLOCK,), -1, jnp.int32), doc_ids])
    starts = (seq + REACH - offsets) * BLOCK
    docs_k = jnp.stack(
        [lax.dynamic_slice_in_dim(docs_pad, starts[w], BLOCK, 0) for w in range(4)]
    )
    docs_q = docs_k[3:4]
    docs_k = docs_k[:, :, None]

    per = heads // chunks
    outs, grads = [], []
    for c in range(chunks):
        own = gather_heads([key_rows, value_rows], c)
        qg = gather_heads([queries, out_grad], c)
        near = lax.ppermute(own, "seq", odd)
        mid = lax.ppermute(own, "seq", two)
        far = lax.ppermute(mid, "seq", mate)
        out, parts = attention(
            slots[:, c * per : (c + 1) * per], docs_q, docs_k, qg, own, near, mid, far
        )
        outs.append(give_tokens(out))
        swapped = lax.ppermute(parts[2], "seq", back(mate))
        from_near = lax.ppermute(parts[0], "seq", back(odd))
        joined = (parts[1].astype(jnp.float32) + swapped.astype(jnp.float32)).astype(jnp.bfloat16)
        from_mid = lax.ppermute(joined, "seq", back(two))
        total = (
            parts[3].astype(jnp.float32)
            + from_near.astype(jnp.float32)
            + from_mid.astype(jnp.float32)
        ).astype(jnp.bfloat16)
        grads.append(give_tokens(total))

    def whole(pieces, which):
        x = jnp.stack([p[which] for p in pieces], axis=2)
        return x.reshape(rows, peers * width)

    return (whole(outs, 0), whole(outs, 1), whole(grads, 0), whole(grads, 1))


def solution(mesh):
    tokens = P(("seq", "head"), None)
    return jax.shard_map(
        per_device,
        mesh=mesh,
        in_specs=(tokens, tokens, tokens, tokens, P(), P("seq", "head", None)),
        out_specs=(tokens, tokens, tokens, tokens),
        check_vma=False,
    )
```

```python
import functools
import jax
import jax.numpy as jnp
from jax import lax
from jax.experimental import pallas as pl
from jax.experimental.pallas import tpu as pltpu
from jax.sharding import PartitionSpec as P

HEAD_DIM = 128
BLOCK = 512
REACH = 3
NEGATIVE = -1e30
CHUNKS = 2
AHEAD = 2
LAGS = (2, 3, 4, 6)


def nt(a, b):
    return lax.dot_general(a, b, (((1,), (1,)), ((), ())), preferred_element_type=jnp.float32)


def nn(a, b):
    return lax.dot_general(a, b, (((1,), (0,)), ((), ())), preferred_element_type=jnp.float32)


def one_head(q, g, keys, values, biases):
    scale = HEAD_DIM**-0.5
    scores = [nt(k, q) * scale + b for k, b in zip(keys, biases)]
    top = functools.reduce(
        jnp.maximum, [jnp.max(s, axis=0, keepdims=True) for s in scores]
    )
    exps = [jnp.exp(s - top) for s in scores]
    total = functools.reduce(jnp.add, [jnp.sum(e, axis=0, keepdims=True) for e in exps])
    inverse = 1.0 / total
    probs = [e * inverse for e in exps]
    lows = [p.astype(jnp.bfloat16) for p in probs]
    out_t = functools.reduce(
        jnp.add, [nn(v.T, p) for v, p in zip(values, lows)]
    )
    out_low = out_t.astype(jnp.bfloat16)
    g_t = g.astype(jnp.float32).T
    delta = jnp.sum(out_low.astype(jnp.float32) * g_t, axis=0, keepdims=True)
    grads = [
        (p * (nt(v, g) - delta)).astype(jnp.bfloat16) for p, v in zip(probs, values)
    ]
    dq_t = functools.reduce(jnp.add, [nn(k.T, d) for k, d in zip(keys, grads)]) * scale
    dks = [nn(d, q) * scale for d in grads]
    dvs = [nn(p, g) for p in lows]
    return out_t.T.astype(jnp.bfloat16), dq_t.T.astype(jnp.bfloat16), dks, dvs


def attend(slots, docs_q, docs_k, qg, own, near, mid, far, out, parts, bias):
    i = pl.program_id(0)

    @pl.when(i == 0)
    def _():
        rows = lax.broadcasted_iota(jnp.int32, (BLOCK, BLOCK), 0)
        cols = lax.broadcasted_iota(jnp.int32, (BLOCK, BLOCK), 1)
        for w in range(4):
            ok = docs_k[w] == docs_q[...]
            if w == 3:
                ok = jnp.logical_and(ok, rows <= cols)
            bias[w] = jnp.where(ok, 0.0, NEGATIVE)

    a, b = slots[0, i], slots[1, i]

    def pick(n, which):
        return jnp.where(n == 0, near[which], jnp.where(n == 1, mid[which], far[which]))

    keys = [pick(a, 0), pick(b, 0), own[0]]
    values = [pick(a, 1), pick(b, 1), own[1]]
    biases = [bias[a], bias[b], bias[3]]
    o, dq, dks, dvs = one_head(qg[0], qg[1], keys, values, biases)
    out[0] = o
    out[1] = dq
    for which, d in ((0, dks), (1, dvs)):
        parts[3, which] = d[2].astype(jnp.bfloat16)
        for w in range(3):
            here = jnp.where(a == w, d[0], jnp.where(b == w, d[1], 0.0))
            parts[w, which] = here.astype(jnp.bfloat16)


def attention(slots, docs_q, docs_k, qg, own, near, mid, far):
    heads = qg.shape[2] // HEAD_DIM
    pair = pl.BlockSpec((2, BLOCK, HEAD_DIM), lambda i, *_: (0, 0, i))
    width = qg.shape[2]
    return pl.pallas_call(
        attend,
        grid_spec=pltpu.PrefetchScalarGridSpec(
            num_scalar_prefetch=1,
            grid=(heads,),
            in_specs=[
                pl.BlockSpec((1, BLOCK), lambda i, *_: (0, 0)),
                pl.BlockSpec((4, BLOCK, 1), lambda i, *_: (0, 0, 0)),
                pair,
                pair,
                pair,
                pair,
                pair,
            ],
            out_specs=[
                pair,
                pl.BlockSpec((4, 2, BLOCK, HEAD_DIM), lambda i, *_: (0, 0, 0, i)),
            ],
            scratch_shapes=[pltpu.VMEM((4, BLOCK, BLOCK), jnp.float32)],
        ),
        out_shape=[
            jax.ShapeDtypeStruct((2, BLOCK, width), jnp.bfloat16),
            jax.ShapeDtypeStruct((4, 2, BLOCK, width), jnp.bfloat16),
        ],
        compiler_params=pltpu.CompilerParams(
            dimension_semantics=("arbitrary",), vmem_limit_bytes=50 * 2**20
        ),
        cost_estimate=pl.CostEstimate(
            flops=heads * 12 * 128 * 512 * 1536 * 3,
            bytes_accessed=20 * BLOCK * width * 2,
            transcendentals=heads * 512 * 1536,
        ),
    )(slots, docs_q, docs_k, qg, own, near, mid, far)


def whole_pass(peers, length, slots, docs_q, docs_k, q_ref, k_ref, v_ref, g_ref,
               o_out, dq_out, dk_out, dv_out,
               own, near, mid, far, mate_back, near_back, mid_back, bias,
               in_send, in_recv, in_local, near_send, near_recv, mid_send, mid_recv,
               far_send, far_recv, back_send, mate_back_recv, near_back_recv, mid_back_recv,
               out_send, out_recv, out_local):
    seq = lax.axis_index("seq")
    rank = lax.axis_index("head")
    other = 1 - rank
    heads = own.shape[0]
    rows = q_ref.shape[0]
    width = heads * HEAD_DIM
    parity = lax.rem(seq, 2)
    even = parity == 0
    mate = seq + 1 - 2 * parity
    has_before = seq >= 2
    has_after = seq + 2 < length
    near_to = jnp.where(even, seq + 1, seq + 3)
    near_from = jnp.where(even, seq - 3, seq - 1)
    near_goes = near_to < length
    near_comes = near_from >= 0
    sources = (k_ref, v_ref, q_ref, g_ref)
    results = (dk_out, dv_out, o_out, dq_out)

    def copy(src, dst, send, recv, where):
        return pltpu.make_async_remote_copy(
            src_ref=src, dst_ref=dst, send_sem=send, recv_sem=recv,
            device_id=where, device_id_type=pl.DeviceIdType.MESH,
        )

    def token_rows(r):
        return pl.ds(pl.multiple_of(r * rows, rows), rows)

    def columns(r, g):
        return pl.ds(pl.multiple_of(r * width + g * HEAD_DIM, HEAD_DIM), HEAD_DIM)

    def group(r):
        return pl.ds(pl.multiple_of(r * width, width), width)

    def in_copy(a, g):
        return copy(sources[a].at[:, columns(other, g)], own.at[g, a, token_rows(rank), :],
                    in_send.at[a], in_recv.at[a, g], (seq, other))

    def in_arrival(a, g):
        return copy(sources[a].at[:, columns(other, g)], own.at[g, a, token_rows(other), :],
                    in_send.at[a], in_recv.at[a, g], (seq, other))

    def in_stay(a, g):
        return pltpu.make_async_copy(sources[a].at[:, columns(rank, g)],
                                     own.at[g, a, token_rows(rank), :], in_local.at[a, g])

    def near_copy(g):
        return copy(own.at[g, pl.ds(0, 2)], near.at[g], near_send.at[g], near_recv.at[g],
                    (near_to, rank))

    def mid_copy(g):
        return copy(own.at[g, pl.ds(0, 2)], mid.at[g], mid_send.at[g], mid_recv.at[g],
                    (seq + 2, rank))

    def far_copy(g):
        return copy(mid.at[g], far.at[g], far_send.at[g], far_recv.at[g], (mate, rank))

    def mate_back_copy(g):
        return copy(far.at[g], mate_back.at[g], back_send.at[0], mate_back_recv.at[g],
                    (mate, rank))

    def near_back_copy(g):
        return copy(near.at[g], near_back.at[g], back_send.at[1], near_back_recv.at[g],
                    (near_from, rank))

    def mid_back_copy(g):
        return copy(mid.at[g], mid_back.at[g], back_send.at[2], mid_back_recv.at[g],
                    (seq - 2, rank))

    def out_copy(a, g):
        return copy(own.at[g, a, token_rows(other), :], results[a].at[:, columns(rank, g)],
                    out_send.at[a], out_recv.at[a], (seq, other))

    def out_stay(a, g):
        return pltpu.make_async_copy(own.at[g, a, token_rows(rank), :],
                                     results[a].at[:, columns(rank, g)], out_local.at[a])

    barrier = pltpu.get_barrier_semaphore()

    def greet(where):
        pl.semaphore_signal(barrier, inc=1, device_id=where,
                            device_id_type=pl.DeviceIdType.MESH)

    greet((seq, other))
    greet((mate, rank))

    @pl.when(has_before)
    def _():
        greet((seq - 2, rank))

    @pl.when(has_after)
    def _():
        greet((seq + 2, rank))

    @pl.when(jnp.logical_and(even, near_comes))
    def _():
        greet((near_from, rank))

    @pl.when(jnp.logical_and(jnp.logical_not(even), near_goes))
    def _():
        greet((near_to, rank))

    across = jnp.where(even, near_comes, near_goes)
    pl.semaphore_wait(
        barrier,
        2 + has_before.astype(jnp.int32) + has_after.astype(jnp.int32) + across.astype(jnp.int32),
    )

    def arrive(g):
        for a in range(4):
            in_copy(a, g).start()
            in_stay(a, g).start()

    for g in range(AHEAD):
        arrive(g)

    def clear(buffer):
        def one(g, _):
            buffer[g] = jnp.zeros(buffer.shape[1:], buffer.dtype)
            return 0

        lax.fori_loop(0, heads, one, 0)

    @pl.when(jnp.logical_not(has_before))
    def _():
        clear(mid)
        clear(far)

    @pl.when(jnp.logical_not(near_comes))
    def _():
        clear(near)

    @pl.when(jnp.logical_not(near_goes))
    def _():
        clear(near_back)

    @pl.when(jnp.logical_not(has_after))
    def _():
        clear(mid_back)

    at_row = lax.broadcasted_iota(jnp.int32, (BLOCK, BLOCK), 0)
    at_col = lax.broadcasted_iota(jnp.int32, (BLOCK, BLOCK), 1)
    for w in range(4):
        ok = docs_k[w] == docs_q[...]
        if w == 3:
            ok = jnp.logical_and(ok, at_row <= at_col)
        bias[w] = jnp.where(ok, 0.0, NEGATIVE)

    def spread(g):
        for a in range(2):
            in_arrival(a, g).wait_recv()
            in_stay(a, g).wait()

        @pl.when(has_after)
        def _():
            mid_copy(g).start()

        @pl.when(near_goes)
        def _():
            near_copy(g).start()

    def forward(g):
        @pl.when(has_before)
        def _():
            mid_copy(g).wait_recv()
            far_copy(g).start()

    def compute(g):
        for a in range(2, 4):
            in_arrival(a, g).wait_recv()
            in_stay(a, g).wait()

        @pl.when(near_comes)
        def _():
            near_copy(g).wait_recv()

        @pl.when(has_before)
        def _():
            far_copy(g).wait_recv()
            far_copy(g).wait_send()

        @pl.when(has_after)
        def _():
            mid_copy(g).wait_send()

        @pl.when(near_goes)
        def _():
            near_copy(g).wait_send()

        a, b = slots[0, g], slots[1, g]

        def pick(n, which):
            return jnp.where(
                n == 0, near[g, which], jnp.where(n == 1, mid[g, which], far[g, which])
            )

        keys = [pick(a, 0), pick(b, 0), own[g, 0]]
        values = [pick(a, 1), pick(b, 1), own[g, 1]]
        biases = [bias[a], bias[b], bias[3]]
        o, dq, dks, dvs = one_head(own[g, 2], own[g, 3], keys, values, biases)
        own[g, 2] = o
        own[g, 3] = dq
        for which, d in ((0, dks), (1, dvs)):
            own[g, which] = d[2].astype(jnp.bfloat16)
            for w, buffer in enumerate((near, mid, far)):
                here = jnp.where(a == w, d[0], jnp.where(b == w, d[1], 0.0))
                buffer[g, which] = here.astype(jnp.bfloat16)

        @pl.when(has_before)
        def _():
            mate_back_copy(g).start()

        @pl.when(near_comes)
        def _():
            near_back_copy(g).start()

        for a in range(2, 4):
            out_copy(a, g).start()
            out_stay(a, g).start()

    def join(g):
        @pl.when(has_before)
        def _():
            mate_back_copy(g).wait_recv()
            both = mid[g].astype(jnp.float32) + mate_back[g].astype(jnp.float32)
            mid[g] = both.astype(jnp.bfloat16)
            mid_back_copy(g).start()

    def finish(g):
        @pl.when(near_goes)
        def _():
            near_back_copy(g).wait_recv()

        @pl.when(has_after)
        def _():
            mid_back_copy(g).wait_recv()

        total = (
            own[g, pl.ds(0, 2)].astype(jnp.float32)
            + near_back[g].astype(jnp.float32)
            + mid_back[g].astype(jnp.float32)
        )
        own[g, pl.ds(0, 2)] = total.astype(jnp.bfloat16)
        for a in range(2):
            out_copy(a, g).start()
            out_stay(a, g).start()

    stages = ((arrive, -AHEAD), (spread, 0), (forward, LAGS[0]), (join, LAGS[2]),
              (finish, LAGS[3]), (compute, LAGS[1]))

    def step(t, _):
        for stage, lag in stages:
            g = t - lag

            @pl.when(jnp.logical_and(g >= 0, g < heads))
            def _():
                stage(g)

        return 0

    lax.fori_loop(0, heads + LAGS[3], step, 0)

    def drain(view, semaphore):
        pltpu.make_async_copy(view, view, semaphore).wait()

    for a in range(4):
        drain(sources[a].at[:, group(other)], in_send.at[a])
        drain(results[a].at[:, group(rank)], out_send.at[a])
        drain(results[a].at[:, group(rank)], out_local.at[a])
        drain(results[a].at[:, group(other)], out_recv.at[a])

    @pl.when(has_before)
    def _():
        drain(far, back_send.at[0])
        drain(mid, back_send.at[2])

    @pl.when(near_comes)
    def _():
        drain(near, back_send.at[1])


def whole_call(peers, length, slots, docs_q, docs_k, queries, key_rows, value_rows, out_grad):
    heads = queries.shape[1] // peers // HEAD_DIM
    window = pltpu.VMEM((heads, 2, BLOCK, HEAD_DIM), jnp.bfloat16)
    dma = pltpu.SemaphoreType.DMA
    hbm = pl.BlockSpec(memory_space=pl.ANY)
    vmem = pl.BlockSpec(memory_space=pltpu.VMEM)
    result = jax.ShapeDtypeStruct(queries.shape, jnp.bfloat16)
    return pl.pallas_call(
        functools.partial(whole_pass, peers, length),
        in_specs=[pl.BlockSpec(memory_space=pltpu.SMEM), vmem, vmem, hbm, hbm, hbm, hbm],
        out_specs=[hbm] * 4,
        out_shape=[result] * 4,
        scratch_shapes=[pltpu.VMEM((heads, 4, BLOCK, HEAD_DIM), jnp.bfloat16)]
        + [window] * 6
        + [pltpu.VMEM((4, BLOCK, BLOCK), jnp.float32)]
        + [dma((4,)), dma((4, heads)), dma((4, heads))]
        + [dma((heads,))] * 6
        + [dma((3,))]
        + [dma((heads,))] * 3
        + [dma((4,))] * 3,
        compiler_params=pltpu.CompilerParams(
            collective_id=0, has_side_effects=True, vmem_limit_bytes=60 * 2**20
        ),
        cost_estimate=pl.CostEstimate(
            flops=heads * 12 * 128 * 512 * 1536,
            bytes_accessed=16 * 2**20,
            transcendentals=heads * 512 * 1536,
        ),
    )(slots, docs_q, docs_k, queries, key_rows, value_rows, out_grad)


def per_device(queries, key_rows, value_rows, out_grad, doc_ids, picks):
    peers = lax.axis_size("head")
    length = lax.axis_size("seq")
    seq = lax.axis_index("seq")
    rank = lax.axis_index("head")
    rows = queries.shape[0]
    width = queries.shape[1] // peers
    heads = width // HEAD_DIM
    chunks = CHUNKS
    part = width // chunks

    def gather_heads(arrays, c):
        x = jnp.stack(arrays)

        if peers != 2:
            x = x.reshape(2, rows, peers, width)[..., c * part : (c + 1) * part]
            x = lax.all_to_all(x, "head", split_axis=2, concat_axis=1, tiled=True)
            return x.reshape(2, rows * peers, part)

        def columns(r):
            return lax.dynamic_slice_in_dim(x, r * width + c * part, part, 2)

        mine = columns(rank)
        theirs = lax.ppermute(columns(1 - rank), "head", [(0, 1), (1, 0)])
        return jnp.where(
            rank == 0,
            jnp.concatenate([mine, theirs], axis=1),
            jnp.concatenate([theirs, mine], axis=1),
        )

    def give_tokens(x):
        if peers != 2:
            x = lax.all_to_all(x, "head", split_axis=1, concat_axis=2, tiled=True)
            return x.reshape(2, rows, peers, part)

        def tokens(r):
            return lax.dynamic_slice_in_dim(x, r * rows, rows, 1)

        mine = tokens(rank)
        theirs = lax.ppermute(tokens(1 - rank), "head", [(0, 1), (1, 0)])
        return jnp.where(
            rank == 0,
            jnp.stack([mine, theirs], axis=2),
            jnp.stack([theirs, mine], axis=2),
        )

    def inside(pairs):
        return [(a, b) for a, b in pairs if 0 <= a < length and 0 <= b < length]

    two = inside([(s, s + 2) for s in range(length)])
    odd = inside([(s, s + 1 if s % 2 == 0 else s + 3) for s in range(length)])
    mate = inside([(s, s ^ 1) for s in range(length)])

    def back(pairs):
        return [(b, a) for a, b in pairs]

    parity = seq % 2
    local = picks[0].T
    slots = jnp.where(local == 2, 1, jnp.where((local == 1) == (parity == 1), 0, 2))
    offsets = jnp.stack(
        [jnp.where(parity == 1, 1, 3), jnp.int32(2), jnp.where(parity == 1, 3, 1), jnp.int32(0)]
    )
    docs_pad = jnp.concatenate([jnp.full((REACH * BLOCK,), -1, jnp.int32), doc_ids])
    starts = (seq + REACH - offsets) * BLOCK
    docs_k = jnp.stack(
        [lax.dynamic_slice_in_dim(docs_pad, starts[w], BLOCK, 0) for w in range(4)]
    )
    docs_q = docs_k[3:4]
    docs_k = docs_k[:, :, None]

    if peers == 2 and length % 2 == 0:
        return whole_call(
            peers, length, slots, docs_q, docs_k, queries, key_rows, value_rows, out_grad
        )

    per = heads // chunks
    outs, grads = [], []
    for c in range(chunks):
        own = gather_heads([key_rows, value_rows], c)
        qg = gather_heads([queries, out_grad], c)
        near = lax.ppermute(own, "seq", odd)
        mid = lax.ppermute(own, "seq", two)
        far = lax.ppermute(mid, "seq", mate)
        out, parts = attention(
            slots[:, c * per : (c + 1) * per], docs_q, docs_k, qg, own, near, mid, far
        )
        outs.append(give_tokens(out))
        swapped = lax.ppermute(parts[2], "seq", back(mate))
        from_near = lax.ppermute(parts[0], "seq", back(odd))
        joined = (parts[1].astype(jnp.float32) + swapped.astype(jnp.float32)).astype(jnp.bfloat16)
        from_mid = lax.ppermute(joined, "seq", back(two))
        total = (
            parts[3].astype(jnp.float32)
            + from_near.astype(jnp.float32)
            + from_mid.astype(jnp.float32)
        ).astype(jnp.bfloat16)
        grads.append(give_tokens(total))

    def whole(pieces, which):
        x = jnp.stack([p[which] for p in pieces], axis=2)
        return x.reshape(rows, peers * width)

    return (whole(outs, 0), whole(outs, 1), whole(grads, 0), whole(grads, 1))


def solution(mesh):
    tokens = P(("seq", "head"), None)
    return jax.shard_map(
        per_device,
        mesh=mesh,
        in_specs=(tokens, tokens, tokens, tokens, P(), P("seq", "head", None)),
        out_specs=(tokens, tokens, tokens, tokens),
        check_vma=False,
    )
```

```python
import functools
import jax
import jax.numpy as jnp
from jax import lax
from jax.experimental import pallas as pl
from jax.experimental.pallas import tpu as pltpu
from jax.sharding import PartitionSpec as P

HEAD_DIM = 128
BLOCK = 512
REACH = 3
NEGATIVE = -1e30
CHUNKS = 2
AHEAD = 4
LAGS = (2, 4, 5, 7)


def nt(a, b):
    return lax.dot_general(a, b, (((1,), (1,)), ((), ())), preferred_element_type=jnp.float32)


def nn(a, b):
    return lax.dot_general(a, b, (((1,), (0,)), ((), ())), preferred_element_type=jnp.float32)


def one_head(q, g, keys, values, biases):
    scale = HEAD_DIM**-0.5
    scores = [nt(k, q) * scale + b for k, b in zip(keys, biases)]
    top = functools.reduce(
        jnp.maximum, [jnp.max(s, axis=0, keepdims=True) for s in scores]
    )
    exps = [jnp.exp(s - top) for s in scores]
    total = functools.reduce(jnp.add, [jnp.sum(e, axis=0, keepdims=True) for e in exps])
    inverse = 1.0 / total
    probs = [e * inverse for e in exps]
    lows = [p.astype(jnp.bfloat16) for p in probs]
    out_t = functools.reduce(
        jnp.add, [nn(v.T, p) for v, p in zip(values, lows)]
    )
    out_low = out_t.astype(jnp.bfloat16)
    g_t = g.astype(jnp.float32).T
    delta = jnp.sum(out_low.astype(jnp.float32) * g_t, axis=0, keepdims=True)
    grads = [
        (p * (nt(v, g) - delta)).astype(jnp.bfloat16) for p, v in zip(probs, values)
    ]
    dq_t = functools.reduce(jnp.add, [nn(k.T, d) for k, d in zip(keys, grads)]) * scale
    dks = [nn(d, q) * scale for d in grads]
    dvs = [nn(p, g) for p in lows]
    return out_t.T.astype(jnp.bfloat16), dq_t.T.astype(jnp.bfloat16), dks, dvs


def attend(slots, docs_q, docs_k, qg, own, near, mid, far, out, parts, bias):
    i = pl.program_id(0)

    @pl.when(i == 0)
    def _():
        rows = lax.broadcasted_iota(jnp.int32, (BLOCK, BLOCK), 0)
        cols = lax.broadcasted_iota(jnp.int32, (BLOCK, BLOCK), 1)
        for w in range(4):
            ok = docs_k[w] == docs_q[...]
            if w == 3:
                ok = jnp.logical_and(ok, rows <= cols)
            bias[w] = jnp.where(ok, 0.0, NEGATIVE)

    a, b = slots[0, i], slots[1, i]

    def pick(n, which):
        return jnp.where(n == 0, near[which], jnp.where(n == 1, mid[which], far[which]))

    keys = [pick(a, 0), pick(b, 0), own[0]]
    values = [pick(a, 1), pick(b, 1), own[1]]
    biases = [bias[a], bias[b], bias[3]]
    o, dq, dks, dvs = one_head(qg[0], qg[1], keys, values, biases)
    out[0] = o
    out[1] = dq
    for which, d in ((0, dks), (1, dvs)):
        parts[3, which] = d[2].astype(jnp.bfloat16)
        for w in range(3):
            here = jnp.where(a == w, d[0], jnp.where(b == w, d[1], 0.0))
            parts[w, which] = here.astype(jnp.bfloat16)


def attention(slots, docs_q, docs_k, qg, own, near, mid, far):
    heads = qg.shape[2] // HEAD_DIM
    pair = pl.BlockSpec((2, BLOCK, HEAD_DIM), lambda i, *_: (0, 0, i))
    width = qg.shape[2]
    return pl.pallas_call(
        attend,
        grid_spec=pltpu.PrefetchScalarGridSpec(
            num_scalar_prefetch=1,
            grid=(heads,),
            in_specs=[
                pl.BlockSpec((1, BLOCK), lambda i, *_: (0, 0)),
                pl.BlockSpec((4, BLOCK, 1), lambda i, *_: (0, 0, 0)),
                pair,
                pair,
                pair,
                pair,
                pair,
            ],
            out_specs=[
                pair,
                pl.BlockSpec((4, 2, BLOCK, HEAD_DIM), lambda i, *_: (0, 0, 0, i)),
            ],
            scratch_shapes=[pltpu.VMEM((4, BLOCK, BLOCK), jnp.float32)],
        ),
        out_shape=[
            jax.ShapeDtypeStruct((2, BLOCK, width), jnp.bfloat16),
            jax.ShapeDtypeStruct((4, 2, BLOCK, width), jnp.bfloat16),
        ],
        compiler_params=pltpu.CompilerParams(
            dimension_semantics=("arbitrary",), vmem_limit_bytes=50 * 2**20
        ),
        cost_estimate=pl.CostEstimate(
            flops=heads * 12 * 128 * 512 * 1536 * 3,
            bytes_accessed=20 * BLOCK * width * 2,
            transcendentals=heads * 512 * 1536,
        ),
    )(slots, docs_q, docs_k, qg, own, near, mid, far)


def whole_pass(peers, length, picks, docs, q_ref, k_ref, v_ref, g_ref,
               o_out, dq_out, dk_out, dv_out,
               own, near, mid, far, mate_back, near_back, mid_back, bias,
               in_send, in_recv, in_local, near_send, near_recv, mid_send, mid_recv,
               far_send, far_recv, back_send, mate_back_recv, near_back_recv, mid_back_recv,
               out_send, out_recv, out_local):
    seq = lax.axis_index("seq")
    rank = lax.axis_index("head")
    other = 1 - rank
    heads = own.shape[0]
    rows = q_ref.shape[0]
    width = heads * HEAD_DIM
    parity = lax.rem(seq, 2)
    even = parity == 0
    mate = seq + 1 - 2 * parity
    has_before = seq >= 2
    has_after = seq + 2 < length
    near_to = jnp.where(even, seq + 1, seq + 3)
    near_from = jnp.where(even, seq - 3, seq - 1)
    near_goes = near_to < length
    near_comes = near_from >= 0
    sources = (k_ref, v_ref, q_ref, g_ref)
    results = (dk_out, dv_out, o_out, dq_out)

    def copy(src, dst, send, recv, where):
        return pltpu.make_async_remote_copy(
            src_ref=src, dst_ref=dst, send_sem=send, recv_sem=recv,
            device_id=where, device_id_type=pl.DeviceIdType.MESH,
        )

    def token_rows(r):
        return pl.ds(pl.multiple_of(r * rows, rows), rows)

    def columns(r, g):
        return pl.ds(pl.multiple_of(r * width + g * HEAD_DIM, HEAD_DIM), HEAD_DIM)

    def group(r):
        return pl.ds(pl.multiple_of(r * width, width), width)

    def in_copy(a, g):
        return copy(sources[a].at[:, columns(other, g)], own.at[g, a, token_rows(rank), :],
                    in_send.at[a], in_recv.at[a, g], (seq, other))

    def in_arrival(a, g):
        return copy(sources[a].at[:, columns(other, g)], own.at[g, a, token_rows(other), :],
                    in_send.at[a], in_recv.at[a, g], (seq, other))

    def in_stay(a, g):
        return pltpu.make_async_copy(sources[a].at[:, columns(rank, g)],
                                     own.at[g, a, token_rows(rank), :], in_local.at[a, g])

    def near_copy(g):
        return copy(own.at[g, pl.ds(0, 2)], near.at[g], near_send.at[g], near_recv.at[g],
                    (near_to, rank))

    def mid_copy(g):
        return copy(own.at[g, pl.ds(0, 2)], mid.at[g], mid_send.at[g], mid_recv.at[g],
                    (seq + 2, rank))

    def far_copy(g):
        return copy(mid.at[g], far.at[g], far_send.at[g], far_recv.at[g], (mate, rank))

    def mate_back_copy(g):
        return copy(far.at[g], mate_back.at[g], back_send.at[0], mate_back_recv.at[g],
                    (mate, rank))

    def near_back_copy(g):
        return copy(near.at[g], near_back.at[g], back_send.at[1], near_back_recv.at[g],
                    (near_from, rank))

    def mid_back_copy(g):
        return copy(mid.at[g], mid_back.at[g], back_send.at[2], mid_back_recv.at[g],
                    (seq - 2, rank))

    def out_copy(a, g):
        return copy(own.at[g, a, token_rows(other), :], results[a].at[:, columns(rank, g)],
                    out_send.at[a], out_recv.at[a], (seq, other))

    def out_stay(a, g):
        return pltpu.make_async_copy(own.at[g, a, token_rows(rank), :],
                                     results[a].at[:, columns(rank, g)], out_local.at[a])

    barrier = pltpu.get_barrier_semaphore()

    def greet(where):
        pl.semaphore_signal(barrier, inc=1, device_id=where,
                            device_id_type=pl.DeviceIdType.MESH)

    greet((seq, other))
    greet((mate, rank))

    @pl.when(has_before)
    def _():
        greet((seq - 2, rank))

    @pl.when(has_after)
    def _():
        greet((seq + 2, rank))

    @pl.when(jnp.logical_and(even, near_comes))
    def _():
        greet((near_from, rank))

    @pl.when(jnp.logical_and(jnp.logical_not(even), near_goes))
    def _():
        greet((near_to, rank))

    across = jnp.where(even, near_comes, near_goes)
    pl.semaphore_wait(
        barrier,
        2 + has_before.astype(jnp.int32) + has_after.astype(jnp.int32) + across.astype(jnp.int32),
    )

    def arrive(g):
        for a in range(2):
            in_copy(a, g).start()
            in_stay(a, g).start()

    def follow(g):
        for a in range(2, 4):
            in_copy(a, g).start()
            in_stay(a, g).start()

    for g in range(AHEAD):
        arrive(g)
    follow(0)

    def clear(buffer):
        def one(g, _):
            buffer[g] = jnp.zeros(buffer.shape[1:], buffer.dtype)
            return 0

        lax.fori_loop(0, heads, one, 0)

    @pl.when(jnp.logical_not(has_before))
    def _():
        clear(mid)
        clear(far)

    @pl.when(jnp.logical_not(near_comes))
    def _():
        clear(near)

    @pl.when(jnp.logical_not(near_goes))
    def _():
        clear(near_back)

    @pl.when(jnp.logical_not(has_after))
    def _():
        clear(mid_back)

    offsets = (jnp.where(even, 3, 1), 2, jnp.where(even, 1, 3), 0)
    at_row = lax.broadcasted_iota(jnp.int32, (BLOCK, BLOCK), 0)
    at_col = lax.broadcasted_iota(jnp.int32, (BLOCK, BLOCK), 1)
    for w in range(4):
        block = seq - offsets[w]
        ids = jnp.where(block >= 0, docs[jnp.maximum(block, 0)], -1)
        tall = jnp.broadcast_to(ids.astype(jnp.float32), (HEAD_DIM, BLOCK)).T[:, :1]
        ok = tall == docs[seq].astype(jnp.float32)
        if w == 3:
            ok = jnp.logical_and(ok, at_row <= at_col)
        bias[w] = jnp.where(ok, 0.0, NEGATIVE)

    def slot(pick):
        return jnp.where(pick == 2, 1, jnp.where(pick == offsets[0], 0, 2))

    def spread(g):
        for a in range(2):
            in_arrival(a, g).wait_recv()
            in_stay(a, g).wait()

        @pl.when(has_after)
        def _():
            mid_copy(g).start()

        @pl.when(near_goes)
        def _():
            near_copy(g).start()

    def forward(g):
        @pl.when(has_before)
        def _():
            mid_copy(g).wait_recv()
            far_copy(g).start()

    def compute(g):
        for a in range(2, 4):
            in_arrival(a, g).wait_recv()
            in_stay(a, g).wait()

        @pl.when(near_comes)
        def _():
            near_copy(g).wait_recv()

        @pl.when(has_before)
        def _():
            far_copy(g).wait_recv()
            far_copy(g).wait_send()

        @pl.when(has_after)
        def _():
            mid_copy(g).wait_send()

        @pl.when(near_goes)
        def _():
            near_copy(g).wait_send()

        a, b = slot(picks[0, g, 0]), slot(picks[0, g, 1])

        def pick(n, which):
            return jnp.where(
                n == 0, near[g, which], jnp.where(n == 1, mid[g, which], far[g, which])
            )

        keys = [pick(a, 0), pick(b, 0), own[g, 0]]
        values = [pick(a, 1), pick(b, 1), own[g, 1]]
        biases = [bias[a], bias[b], bias[3]]
        o, dq, dks, dvs = one_head(own[g, 2], own[g, 3], keys, values, biases)
        own[g, 2] = o
        own[g, 3] = dq
        for which, d in ((0, dks), (1, dvs)):
            own[g, which] = d[2].astype(jnp.bfloat16)
            for w, buffer in enumerate((near, mid, far)):
                here = jnp.where(a == w, d[0], jnp.where(b == w, d[1], 0.0))
                buffer[g, which] = here.astype(jnp.bfloat16)

        @pl.when(has_before)
        def _():
            mate_back_copy(g).start()

        @pl.when(near_comes)
        def _():
            near_back_copy(g).start()

        for a in range(2, 4):
            out_copy(a, g).start()
            out_stay(a, g).start()

    def join(g):
        @pl.when(has_before)
        def _():
            mate_back_copy(g).wait_recv()
            both = mid[g].astype(jnp.float32) + mate_back[g].astype(jnp.float32)
            mid[g] = both.astype(jnp.bfloat16)
            mid_back_copy(g).start()

    def finish(g):
        @pl.when(near_goes)
        def _():
            near_back_copy(g).wait_recv()

        @pl.when(has_after)
        def _():
            mid_back_copy(g).wait_recv()

        total = (
            own[g, pl.ds(0, 2)].astype(jnp.float32)
            + near_back[g].astype(jnp.float32)
            + mid_back[g].astype(jnp.float32)
        )
        own[g, pl.ds(0, 2)] = total.astype(jnp.bfloat16)
        for a in range(2):
            out_copy(a, g).start()
            out_stay(a, g).start()

    stages = ((arrive, -AHEAD), (follow, -1), (spread, 0), (forward, LAGS[0]),
              (compute, LAGS[1]), (join, LAGS[2]), (finish, LAGS[3]))

    def step(t, _):
        for stage, lag in stages:
            g = t - lag

            @pl.when(jnp.logical_and(g >= 0, g < heads))
            def _():
                stage(g)

        return 0

    lax.fori_loop(0, heads + LAGS[3], step, 0)

    def drain(view, semaphore):
        pltpu.make_async_copy(view, view, semaphore).wait()

    for a in range(4):
        drain(sources[a].at[:, group(other)], in_send.at[a])
        drain(results[a].at[:, group(rank)], out_send.at[a])
        drain(results[a].at[:, group(rank)], out_local.at[a])
        drain(results[a].at[:, group(other)], out_recv.at[a])

    @pl.when(has_before)
    def _():
        drain(far, back_send.at[0])
        drain(mid, back_send.at[2])

    @pl.when(near_comes)
    def _():
        drain(near, back_send.at[1])


def whole_call(peers, length, picks, docs, queries, key_rows, value_rows, out_grad):
    heads = queries.shape[1] // peers // HEAD_DIM
    window = pltpu.VMEM((heads, 2, BLOCK, HEAD_DIM), jnp.bfloat16)
    dma = pltpu.SemaphoreType.DMA
    hbm = pl.BlockSpec(memory_space=pl.ANY)
    vmem = pl.BlockSpec(memory_space=pltpu.VMEM)
    result = jax.ShapeDtypeStruct(queries.shape, jnp.bfloat16)
    return pl.pallas_call(
        functools.partial(whole_pass, peers, length),
        in_specs=[pl.BlockSpec(memory_space=pltpu.SMEM), vmem, hbm, hbm, hbm, hbm],
        out_specs=[hbm] * 4,
        out_shape=[result] * 4,
        scratch_shapes=[pltpu.VMEM((heads, 4, BLOCK, HEAD_DIM), jnp.bfloat16)]
        + [window] * 6
        + [pltpu.VMEM((4, BLOCK, BLOCK), jnp.float32)]
        + [dma((4,)), dma((4, heads)), dma((4, heads))]
        + [dma((heads,))] * 6
        + [dma((3,))]
        + [dma((heads,))] * 3
        + [dma((4,))] * 3,
        compiler_params=pltpu.CompilerParams(
            collective_id=0, has_side_effects=True, vmem_limit_bytes=60 * 2**20
        ),
        cost_estimate=pl.CostEstimate(
            flops=heads * 12 * 128 * 512 * 1536,
            bytes_accessed=16 * 2**20,
            transcendentals=heads * 512 * 1536,
        ),
    )(picks, docs, queries, key_rows, value_rows, out_grad)


def per_device(queries, key_rows, value_rows, out_grad, doc_ids, picks):
    peers = lax.axis_size("head")
    length = lax.axis_size("seq")
    seq = lax.axis_index("seq")
    rank = lax.axis_index("head")
    rows = queries.shape[0]
    width = queries.shape[1] // peers
    heads = width // HEAD_DIM
    chunks = CHUNKS
    part = width // chunks

    def gather_heads(arrays, c):
        x = jnp.stack(arrays)

        if peers != 2:
            x = x.reshape(2, rows, peers, width)[..., c * part : (c + 1) * part]
            x = lax.all_to_all(x, "head", split_axis=2, concat_axis=1, tiled=True)
            return x.reshape(2, rows * peers, part)

        def columns(r):
            return lax.dynamic_slice_in_dim(x, r * width + c * part, part, 2)

        mine = columns(rank)
        theirs = lax.ppermute(columns(1 - rank), "head", [(0, 1), (1, 0)])
        return jnp.where(
            rank == 0,
            jnp.concatenate([mine, theirs], axis=1),
            jnp.concatenate([theirs, mine], axis=1),
        )

    def give_tokens(x):
        if peers != 2:
            x = lax.all_to_all(x, "head", split_axis=1, concat_axis=2, tiled=True)
            return x.reshape(2, rows, peers, part)

        def tokens(r):
            return lax.dynamic_slice_in_dim(x, r * rows, rows, 1)

        mine = tokens(rank)
        theirs = lax.ppermute(tokens(1 - rank), "head", [(0, 1), (1, 0)])
        return jnp.where(
            rank == 0,
            jnp.stack([mine, theirs], axis=2),
            jnp.stack([theirs, mine], axis=2),
        )

    def inside(pairs):
        return [(a, b) for a, b in pairs if 0 <= a < length and 0 <= b < length]

    two = inside([(s, s + 2) for s in range(length)])
    odd = inside([(s, s + 1 if s % 2 == 0 else s + 3) for s in range(length)])
    mate = inside([(s, s ^ 1) for s in range(length)])

    def back(pairs):
        return [(b, a) for a, b in pairs]

    parity = seq % 2
    local = picks[0].T
    slots = jnp.where(local == 2, 1, jnp.where((local == 1) == (parity == 1), 0, 2))
    offsets = jnp.stack(
        [jnp.where(parity == 1, 1, 3), jnp.int32(2), jnp.where(parity == 1, 3, 1), jnp.int32(0)]
    )
    docs_pad = jnp.concatenate([jnp.full((REACH * BLOCK,), -1, jnp.int32), doc_ids])
    starts = (seq + REACH - offsets) * BLOCK
    docs_k = jnp.stack(
        [lax.dynamic_slice_in_dim(docs_pad, starts[w], BLOCK, 0) for w in range(4)]
    )
    docs_q = docs_k[3:4]
    docs_k = docs_k[:, :, None]

    if peers == 2 and length % 2 == 0:
        return whole_call(
            peers, length, picks, doc_ids.reshape(-1, 1, BLOCK), queries, key_rows, value_rows,
            out_grad,
        )

    per = heads // chunks
    outs, grads = [], []
    for c in range(chunks):
        own = gather_heads([key_rows, value_rows], c)
        qg = gather_heads([queries, out_grad], c)
        near = lax.ppermute(own, "seq", odd)
        mid = lax.ppermute(own, "seq", two)
        far = lax.ppermute(mid, "seq", mate)
        out, parts = attention(
            slots[:, c * per : (c + 1) * per], docs_q, docs_k, qg, own, near, mid, far
        )
        outs.append(give_tokens(out))
        swapped = lax.ppermute(parts[2], "seq", back(mate))
        from_near = lax.ppermute(parts[0], "seq", back(odd))
        joined = (parts[1].astype(jnp.float32) + swapped.astype(jnp.float32)).astype(jnp.bfloat16)
        from_mid = lax.ppermute(joined, "seq", back(two))
        total = (
            parts[3].astype(jnp.float32)
            + from_near.astype(jnp.float32)
            + from_mid.astype(jnp.float32)
        ).astype(jnp.bfloat16)
        grads.append(give_tokens(total))

    def whole(pieces, which):
        x = jnp.stack([p[which] for p in pieces], axis=2)
        return x.reshape(rows, peers * width)

    return (whole(outs, 0), whole(outs, 1), whole(grads, 0), whole(grads, 1))


def solution(mesh):
    tokens = P(("seq", "head"), None)
    return jax.shard_map(
        per_device,
        mesh=mesh,
        in_specs=(tokens, tokens, tokens, tokens, P(), P("seq", "head", None)),
        out_specs=(tokens, tokens, tokens, tokens),
        check_vma=False,
    )
```

```python
import functools
import jax
import jax.numpy as jnp
from jax import lax
from jax.experimental import pallas as pl
from jax.experimental.pallas import tpu as pltpu
from jax.sharding import PartitionSpec as P

HEAD_DIM = 128
BLOCK = 512
REACH = 3
NEGATIVE = -1e30
CHUNKS = 2
PAIR = 2 * HEAD_DIM
AHEAD = 4
LAGS = (2, 3, 4, 6)


def nt(a, b):
    return lax.dot_general(a, b, (((1,), (1,)), ((), ())), preferred_element_type=jnp.float32)


def nn(a, b):
    return lax.dot_general(a, b, (((1,), (0,)), ((), ())), preferred_element_type=jnp.float32)


def one_head(q, g, keys, values, biases):
    scale = HEAD_DIM**-0.5
    scores = [nt(k, q) * scale + b for k, b in zip(keys, biases)]
    top = functools.reduce(
        jnp.maximum, [jnp.max(s, axis=0, keepdims=True) for s in scores]
    )
    exps = [jnp.exp(s - top) for s in scores]
    total = functools.reduce(jnp.add, [jnp.sum(e, axis=0, keepdims=True) for e in exps])
    inverse = 1.0 / total
    probs = [e * inverse for e in exps]
    lows = [p.astype(jnp.bfloat16) for p in probs]
    out_t = functools.reduce(
        jnp.add, [nn(v.T, p) for v, p in zip(values, lows)]
    )
    out_low = out_t.astype(jnp.bfloat16)
    g_t = g.astype(jnp.float32).T
    delta = jnp.sum(out_low.astype(jnp.float32) * g_t, axis=0, keepdims=True)
    grads = [
        (p * (nt(v, g) - delta)).astype(jnp.bfloat16) for p, v in zip(probs, values)
    ]
    dq_t = functools.reduce(jnp.add, [nn(k.T, d) for k, d in zip(keys, grads)]) * scale
    dks = [nn(d, q) * scale for d in grads]
    dvs = [nn(p, g) for p in lows]
    return out_t.T.astype(jnp.bfloat16), dq_t.T.astype(jnp.bfloat16), dks, dvs


def attend(slots, docs_q, docs_k, qg, own, near, mid, far, out, parts, bias):
    i = pl.program_id(0)

    @pl.when(i == 0)
    def _():
        rows = lax.broadcasted_iota(jnp.int32, (BLOCK, BLOCK), 0)
        cols = lax.broadcasted_iota(jnp.int32, (BLOCK, BLOCK), 1)
        for w in range(4):
            ok = docs_k[w] == docs_q[...]
            if w == 3:
                ok = jnp.logical_and(ok, rows <= cols)
            bias[w] = jnp.where(ok, 0.0, NEGATIVE)

    a, b = slots[0, i], slots[1, i]

    def pick(n, which):
        return jnp.where(n == 0, near[which], jnp.where(n == 1, mid[which], far[which]))

    keys = [pick(a, 0), pick(b, 0), own[0]]
    values = [pick(a, 1), pick(b, 1), own[1]]
    biases = [bias[a], bias[b], bias[3]]
    o, dq, dks, dvs = one_head(qg[0], qg[1], keys, values, biases)
    out[0] = o
    out[1] = dq
    for which, d in ((0, dks), (1, dvs)):
        parts[3, which] = d[2].astype(jnp.bfloat16)
        for w in range(3):
            here = jnp.where(a == w, d[0], jnp.where(b == w, d[1], 0.0))
            parts[w, which] = here.astype(jnp.bfloat16)


def attention(slots, docs_q, docs_k, qg, own, near, mid, far):
    heads = qg.shape[2] // HEAD_DIM
    pair = pl.BlockSpec((2, BLOCK, HEAD_DIM), lambda i, *_: (0, 0, i))
    width = qg.shape[2]
    return pl.pallas_call(
        attend,
        grid_spec=pltpu.PrefetchScalarGridSpec(
            num_scalar_prefetch=1,
            grid=(heads,),
            in_specs=[
                pl.BlockSpec((1, BLOCK), lambda i, *_: (0, 0)),
                pl.BlockSpec((4, BLOCK, 1), lambda i, *_: (0, 0, 0)),
                pair,
                pair,
                pair,
                pair,
                pair,
            ],
            out_specs=[
                pair,
                pl.BlockSpec((4, 2, BLOCK, HEAD_DIM), lambda i, *_: (0, 0, 0, i)),
            ],
            scratch_shapes=[pltpu.VMEM((4, BLOCK, BLOCK), jnp.float32)],
        ),
        out_shape=[
            jax.ShapeDtypeStruct((2, BLOCK, width), jnp.bfloat16),
            jax.ShapeDtypeStruct((4, 2, BLOCK, width), jnp.bfloat16),
        ],
        compiler_params=pltpu.CompilerParams(
            dimension_semantics=("arbitrary",), vmem_limit_bytes=50 * 2**20
        ),
        cost_estimate=pl.CostEstimate(
            flops=heads * 12 * 128 * 512 * 1536 * 3,
            bytes_accessed=20 * BLOCK * width * 2,
            transcendentals=heads * 512 * 1536,
        ),
    )(slots, docs_q, docs_k, qg, own, near, mid, far)


def whole_pass(peers, length, picks, docs, q_ref, k_ref, v_ref, g_ref,
               o_out, dq_out, dk_out, dv_out,
               own, near, mid, far, mate_back, near_back, mid_back, bias,
               in_send, in_recv, in_local, near_send, near_recv, mid_send, mid_recv,
               far_send, far_recv, back_send, mate_back_recv, near_back_recv, mid_back_recv,
               out_send, out_recv, out_local):
    seq = lax.axis_index("seq")
    rank = lax.axis_index("head")
    other = 1 - rank
    heads = near.shape[0]
    rows = q_ref.shape[0]
    width = heads * HEAD_DIM
    parity = lax.rem(seq, 2)
    even = parity == 0
    mate = seq + 1 - 2 * parity
    has_before = seq >= 2
    has_after = seq + 2 < length
    near_to = jnp.where(even, seq + 1, seq + 3)
    near_from = jnp.where(even, seq - 3, seq - 1)
    near_goes = near_to < length
    near_comes = near_from >= 0
    sources = (k_ref, v_ref, q_ref, g_ref)
    results = (dk_out, dv_out, o_out, dq_out)

    def copy(src, dst, send, recv, where):
        return pltpu.make_async_remote_copy(
            src_ref=src, dst_ref=dst, send_sem=send, recv_sem=recv,
            device_id=where, device_id_type=pl.DeviceIdType.MESH,
        )

    def token_rows(r):
        return pl.ds(pl.multiple_of(r * rows, rows), rows)

    def columns(r, p):
        return pl.ds(pl.multiple_of(r * width + p * PAIR, PAIR), PAIR)

    def place(g):
        return lax.div(g, 2), pl.ds(pl.multiple_of(lax.rem(g, 2) * HEAD_DIM, HEAD_DIM), HEAD_DIM)

    def own_keys(g):
        p, lanes = place(g)
        return own.at[p, pl.ds(0, 2), :, lanes]

    def on_first(g, act):
        @pl.when(lax.rem(g, 2) == 0)
        def _():
            act(lax.div(g, 2))

    def on_second(g, act):
        @pl.when(lax.rem(g, 2) == 1)
        def _():
            act(lax.div(g, 2))

    def group(r):
        return pl.ds(pl.multiple_of(r * width, width), width)

    def in_copy(a, g):
        return copy(sources[a].at[:, columns(other, g)], own.at[g, a, token_rows(rank), :],
                    in_send.at[a], in_recv.at[a, g], (seq, other))

    def in_arrival(a, g):
        return copy(sources[a].at[:, columns(other, g)], own.at[g, a, token_rows(other), :],
                    in_send.at[a], in_recv.at[a, g], (seq, other))

    def in_stay(a, g):
        return pltpu.make_async_copy(sources[a].at[:, columns(rank, g)],
                                     own.at[g, a, token_rows(rank), :], in_local.at[a, g])

    def near_copy(g):
        return copy(own_keys(g), near.at[g], near_send.at[g], near_recv.at[g],
                    (near_to, rank))

    def mid_copy(g):
        return copy(own_keys(g), mid.at[g], mid_send.at[g], mid_recv.at[g],
                    (seq + 2, rank))

    def far_copy(g):
        return copy(mid.at[g], far.at[g], far_send.at[g], far_recv.at[g], (mate, rank))

    def mate_back_copy(g):
        return copy(far.at[g], mate_back.at[g], back_send.at[0], mate_back_recv.at[g],
                    (mate, rank))

    def near_back_copy(g):
        return copy(near.at[g], near_back.at[g], back_send.at[1], near_back_recv.at[g],
                    (near_from, rank))

    def mid_back_copy(g):
        return copy(mid.at[g], mid_back.at[g], back_send.at[2], mid_back_recv.at[g],
                    (seq - 2, rank))

    def out_copy(a, g):
        return copy(own.at[g, a, token_rows(other), :], results[a].at[:, columns(rank, g)],
                    out_send.at[a], out_recv.at[a], (seq, other))

    def out_stay(a, g):
        return pltpu.make_async_copy(own.at[g, a, token_rows(rank), :],
                                     results[a].at[:, columns(rank, g)], out_local.at[a])

    barrier = pltpu.get_barrier_semaphore()

    def greet(where):
        pl.semaphore_signal(barrier, inc=1, device_id=where,
                            device_id_type=pl.DeviceIdType.MESH)

    greet((seq, other))
    greet((mate, rank))

    @pl.when(has_before)
    def _():
        greet((seq - 2, rank))

    @pl.when(has_after)
    def _():
        greet((seq + 2, rank))

    @pl.when(jnp.logical_and(even, near_comes))
    def _():
        greet((near_from, rank))

    @pl.when(jnp.logical_and(jnp.logical_not(even), near_goes))
    def _():
        greet((near_to, rank))

    across = jnp.where(even, near_comes, near_goes)
    pl.semaphore_wait(
        barrier,
        2 + has_before.astype(jnp.int32) + has_after.astype(jnp.int32) + across.astype(jnp.int32),
    )

    def enter(low):
        def act(p):
            for a in range(low, low + 2):
                in_copy(a, p).start()
                in_stay(a, p).start()

        return act

    def entered(low):
        def act(p):
            for a in range(low, low + 2):
                in_arrival(a, p).wait_recv()
                in_stay(a, p).wait()

        return act

    def leave(low):
        def act(p):
            for a in range(low, low + 2):
                out_copy(a, p).start()
                out_stay(a, p).start()

        return act

    def arrive(g):
        on_first(g, enter(0))

    def follow(g):
        on_first(g, enter(2))

    for p in range(AHEAD // 2):
        enter(0)(p)
    enter(2)(0)

    def clear(buffer):
        def one(g, _):
            buffer[g] = jnp.zeros(buffer.shape[1:], buffer.dtype)
            return 0

        lax.fori_loop(0, heads, one, 0)

    @pl.when(jnp.logical_not(has_before))
    def _():
        clear(mid)
        clear(far)

    @pl.when(jnp.logical_not(near_comes))
    def _():
        clear(near)

    @pl.when(jnp.logical_not(near_goes))
    def _():
        clear(near_back)

    @pl.when(jnp.logical_not(has_after))
    def _():
        clear(mid_back)

    offsets = (jnp.where(even, 3, 1), 2, jnp.where(even, 1, 3), 0)
    at_row = lax.broadcasted_iota(jnp.int32, (BLOCK, BLOCK), 0)
    at_col = lax.broadcasted_iota(jnp.int32, (BLOCK, BLOCK), 1)
    for w in range(4):
        block = seq - offsets[w]
        ids = jnp.where(block >= 0, docs[jnp.maximum(block, 0)], -1)
        tall = jnp.broadcast_to(ids.astype(jnp.float32), (HEAD_DIM, BLOCK)).T[:, :1]
        ok = tall == docs[seq].astype(jnp.float32)
        if w == 3:
            ok = jnp.logical_and(ok, at_row <= at_col)
        bias[w] = jnp.where(ok, 0.0, NEGATIVE)

    def slot(pick):
        return jnp.where(pick == 2, 1, jnp.where(pick == offsets[0], 0, 2))

    def spread(g):
        on_first(g, entered(0))

        @pl.when(has_after)
        def _():
            mid_copy(g).start()

        @pl.when(near_goes)
        def _():
            near_copy(g).start()

    def forward(g):
        @pl.when(has_before)
        def _():
            mid_copy(g).wait_recv()
            far_copy(g).start()

    def compute(g):
        on_first(g, entered(2))

        @pl.when(near_comes)
        def _():
            near_copy(g).wait_recv()

        @pl.when(has_before)
        def _():
            far_copy(g).wait_recv()
            far_copy(g).wait_send()

        @pl.when(has_after)
        def _():
            mid_copy(g).wait_send()

        @pl.when(near_goes)
        def _():
            near_copy(g).wait_send()

        a, b = slot(picks[0, g, 0]), slot(picks[0, g, 1])

        def pick(n, which):
            return jnp.where(
                n == 0, near[g, which], jnp.where(n == 1, mid[g, which], far[g, which])
            )

        p, lanes = place(g)
        keys = [pick(a, 0), pick(b, 0), own[p, 0, :, lanes]]
        values = [pick(a, 1), pick(b, 1), own[p, 1, :, lanes]]
        biases = [bias[a], bias[b], bias[3]]
        o, dq, dks, dvs = one_head(
            own[p, 2, :, lanes], own[p, 3, :, lanes], keys, values, biases
        )
        own[p, 2, :, lanes] = o
        own[p, 3, :, lanes] = dq
        for which, d in ((0, dks), (1, dvs)):
            own[p, which, :, lanes] = d[2].astype(jnp.bfloat16)
            for w, buffer in enumerate((near, mid, far)):
                here = jnp.where(a == w, d[0], jnp.where(b == w, d[1], 0.0))
                buffer[g, which] = here.astype(jnp.bfloat16)

        @pl.when(has_before)
        def _():
            mate_back_copy(g).start()

        @pl.when(near_comes)
        def _():
            near_back_copy(g).start()

        on_second(g, leave(2))

    def join(g):
        @pl.when(has_before)
        def _():
            mate_back_copy(g).wait_recv()
            both = mid[g].astype(jnp.float32) + mate_back[g].astype(jnp.float32)
            mid[g] = both.astype(jnp.bfloat16)
            mid_back_copy(g).start()

    def finish(g):
        @pl.when(near_goes)
        def _():
            near_back_copy(g).wait_recv()

        @pl.when(has_after)
        def _():
            mid_back_copy(g).wait_recv()

        p, lanes = place(g)
        total = (
            own[p, pl.ds(0, 2), :, lanes].astype(jnp.float32)
            + near_back[g].astype(jnp.float32)
            + mid_back[g].astype(jnp.float32)
        )
        own[p, pl.ds(0, 2), :, lanes] = total.astype(jnp.bfloat16)
        on_second(g, leave(0))

    stages = ((arrive, -AHEAD), (follow, -2), (spread, 0), (forward, LAGS[0]),
              (compute, LAGS[1]), (join, LAGS[2]), (finish, LAGS[3]))

    def step(t, _):
        for stage, lag in stages:
            g = t - lag

            @pl.when(jnp.logical_and(g >= 0, g < heads))
            def _():
                stage(g)

        return 0

    lax.fori_loop(0, heads + LAGS[3], step, 0)

    def drain(view, semaphore):
        pltpu.make_async_copy(view, view, semaphore).wait()

    for a in range(4):
        drain(sources[a].at[:, group(other)], in_send.at[a])
        drain(results[a].at[:, group(rank)], out_send.at[a])
        drain(results[a].at[:, group(rank)], out_local.at[a])
        drain(results[a].at[:, group(other)], out_recv.at[a])

    @pl.when(has_before)
    def _():
        drain(far, back_send.at[0])
        drain(mid, back_send.at[2])

    @pl.when(near_comes)
    def _():
        drain(near, back_send.at[1])


def whole_call(peers, length, picks, docs, queries, key_rows, value_rows, out_grad):
    heads = queries.shape[1] // peers // HEAD_DIM
    window = pltpu.VMEM((heads, 2, BLOCK, HEAD_DIM), jnp.bfloat16)
    dma = pltpu.SemaphoreType.DMA
    hbm = pl.BlockSpec(memory_space=pl.ANY)
    vmem = pl.BlockSpec(memory_space=pltpu.VMEM)
    result = jax.ShapeDtypeStruct(queries.shape, jnp.bfloat16)
    return pl.pallas_call(
        functools.partial(whole_pass, peers, length),
        in_specs=[pl.BlockSpec(memory_space=pltpu.SMEM), vmem, hbm, hbm, hbm, hbm],
        out_specs=[hbm] * 4,
        out_shape=[result] * 4,
        scratch_shapes=[pltpu.VMEM((heads // 2, 4, BLOCK, PAIR), jnp.bfloat16)]
        + [window] * 6
        + [pltpu.VMEM((4, BLOCK, BLOCK), jnp.float32)]
        + [dma((4,)), dma((4, heads // 2)), dma((4, heads // 2))]
        + [dma((heads,))] * 6
        + [dma((3,))]
        + [dma((heads,))] * 3
        + [dma((4,))] * 3,
        compiler_params=pltpu.CompilerParams(
            collective_id=0, has_side_effects=True, vmem_limit_bytes=60 * 2**20
        ),
        cost_estimate=pl.CostEstimate(
            flops=heads * 12 * 128 * 512 * 1536,
            bytes_accessed=16 * 2**20,
            transcendentals=heads * 512 * 1536,
        ),
    )(picks, docs, queries, key_rows, value_rows, out_grad)


def per_device(queries, key_rows, value_rows, out_grad, doc_ids, picks):
    peers = lax.axis_size("head")
    length = lax.axis_size("seq")
    seq = lax.axis_index("seq")
    rank = lax.axis_index("head")
    rows = queries.shape[0]
    width = queries.shape[1] // peers
    heads = width // HEAD_DIM
    chunks = CHUNKS
    part = width // chunks

    def gather_heads(arrays, c):
        x = jnp.stack(arrays)

        if peers != 2:
            x = x.reshape(2, rows, peers, width)[..., c * part : (c + 1) * part]
            x = lax.all_to_all(x, "head", split_axis=2, concat_axis=1, tiled=True)
            return x.reshape(2, rows * peers, part)

        def columns(r):
            return lax.dynamic_slice_in_dim(x, r * width + c * part, part, 2)

        mine = columns(rank)
        theirs = lax.ppermute(columns(1 - rank), "head", [(0, 1), (1, 0)])
        return jnp.where(
            rank == 0,
            jnp.concatenate([mine, theirs], axis=1),
            jnp.concatenate([theirs, mine], axis=1),
        )

    def give_tokens(x):
        if peers != 2:
            x = lax.all_to_all(x, "head", split_axis=1, concat_axis=2, tiled=True)
            return x.reshape(2, rows, peers, part)

        def tokens(r):
            return lax.dynamic_slice_in_dim(x, r * rows, rows, 1)

        mine = tokens(rank)
        theirs = lax.ppermute(tokens(1 - rank), "head", [(0, 1), (1, 0)])
        return jnp.where(
            rank == 0,
            jnp.stack([mine, theirs], axis=2),
            jnp.stack([theirs, mine], axis=2),
        )

    def inside(pairs):
        return [(a, b) for a, b in pairs if 0 <= a < length and 0 <= b < length]

    two = inside([(s, s + 2) for s in range(length)])
    odd = inside([(s, s + 1 if s % 2 == 0 else s + 3) for s in range(length)])
    mate = inside([(s, s ^ 1) for s in range(length)])

    def back(pairs):
        return [(b, a) for a, b in pairs]

    parity = seq % 2
    local = picks[0].T
    slots = jnp.where(local == 2, 1, jnp.where((local == 1) == (parity == 1), 0, 2))
    offsets = jnp.stack(
        [jnp.where(parity == 1, 1, 3), jnp.int32(2), jnp.where(parity == 1, 3, 1), jnp.int32(0)]
    )
    docs_pad = jnp.concatenate([jnp.full((REACH * BLOCK,), -1, jnp.int32), doc_ids])
    starts = (seq + REACH - offsets) * BLOCK
    docs_k = jnp.stack(
        [lax.dynamic_slice_in_dim(docs_pad, starts[w], BLOCK, 0) for w in range(4)]
    )
    docs_q = docs_k[3:4]
    docs_k = docs_k[:, :, None]

    if peers == 2 and length % 2 == 0 and heads % 2 == 0:
        return whole_call(
            peers, length, picks, doc_ids.reshape(-1, 1, BLOCK), queries, key_rows, value_rows,
            out_grad,
        )

    per = heads // chunks
    outs, grads = [], []
    for c in range(chunks):
        own = gather_heads([key_rows, value_rows], c)
        qg = gather_heads([queries, out_grad], c)
        near = lax.ppermute(own, "seq", odd)
        mid = lax.ppermute(own, "seq", two)
        far = lax.ppermute(mid, "seq", mate)
        out, parts = attention(
            slots[:, c * per : (c + 1) * per], docs_q, docs_k, qg, own, near, mid, far
        )
        outs.append(give_tokens(out))
        swapped = lax.ppermute(parts[2], "seq", back(mate))
        from_near = lax.ppermute(parts[0], "seq", back(odd))
        joined = (parts[1].astype(jnp.float32) + swapped.astype(jnp.float32)).astype(jnp.bfloat16)
        from_mid = lax.ppermute(joined, "seq", back(two))
        total = (
            parts[3].astype(jnp.float32)
            + from_near.astype(jnp.float32)
            + from_mid.astype(jnp.float32)
        ).astype(jnp.bfloat16)
        grads.append(give_tokens(total))

    def whole(pieces, which):
        x = jnp.stack([p[which] for p in pieces], axis=2)
        return x.reshape(rows, peers * width)

    return (whole(outs, 0), whole(outs, 1), whole(grads, 0), whole(grads, 1))


def solution(mesh):
    tokens = P(("seq", "head"), None)
    return jax.shard_map(
        per_device,
        mesh=mesh,
        in_specs=(tokens, tokens, tokens, tokens, P(), P("seq", "head", None)),
        out_specs=(tokens, tokens, tokens, tokens),
        check_vma=False,
    )
```

```python
import functools
import jax
import jax.numpy as jnp
from jax import lax
from jax.experimental import pallas as pl
from jax.experimental.pallas import tpu as pltpu
from jax.sharding import PartitionSpec as P

HEAD_DIM = 128
BLOCK = 512
REACH = 3
NEGATIVE = -1e30
CHUNKS = 2
AHEAD = 6
LAGS = (3, 6, 7, 9)


def nt(a, b):
    return lax.dot_general(a, b, (((1,), (1,)), ((), ())), preferred_element_type=jnp.float32)


def nn(a, b):
    return lax.dot_general(a, b, (((1,), (0,)), ((), ())), preferred_element_type=jnp.float32)


def one_head(q, g, keys, values, biases):
    scale = HEAD_DIM**-0.5
    scores = [nt(k, q) * scale + b for k, b in zip(keys, biases)]
    top = functools.reduce(
        jnp.maximum, [jnp.max(s, axis=0, keepdims=True) for s in scores]
    )
    exps = [jnp.exp(s - top) for s in scores]
    total = functools.reduce(jnp.add, [jnp.sum(e, axis=0, keepdims=True) for e in exps])
    inverse = 1.0 / total
    probs = [e * inverse for e in exps]
    lows = [p.astype(jnp.bfloat16) for p in probs]
    out_t = functools.reduce(
        jnp.add, [nn(v.T, p) for v, p in zip(values, lows)]
    )
    out_low = out_t.astype(jnp.bfloat16)
    g_t = g.astype(jnp.float32).T
    delta = jnp.sum(out_low.astype(jnp.float32) * g_t, axis=0, keepdims=True)
    grads = [
        (p * (nt(v, g) - delta)).astype(jnp.bfloat16) for p, v in zip(probs, values)
    ]
    dq_t = functools.reduce(jnp.add, [nn(k.T, d) for k, d in zip(keys, grads)]) * scale
    dks = [nn(d, q) * scale for d in grads]
    dvs = [nn(p, g) for p in lows]
    return out_t.T.astype(jnp.bfloat16), dq_t.T.astype(jnp.bfloat16), dks, dvs


def attend(slots, docs_q, docs_k, qg, own, near, mid, far, out, parts, bias):
    i = pl.program_id(0)

    @pl.when(i == 0)
    def _():
        rows = lax.broadcasted_iota(jnp.int32, (BLOCK, BLOCK), 0)
        cols = lax.broadcasted_iota(jnp.int32, (BLOCK, BLOCK), 1)
        for w in range(4):
            ok = docs_k[w] == docs_q[...]
            if w == 3:
                ok = jnp.logical_and(ok, rows <= cols)
            bias[w] = jnp.where(ok, 0.0, NEGATIVE)

    a, b = slots[0, i], slots[1, i]

    def pick(n, which):
        return jnp.where(n == 0, near[which], jnp.where(n == 1, mid[which], far[which]))

    keys = [pick(a, 0), pick(b, 0), own[0]]
    values = [pick(a, 1), pick(b, 1), own[1]]
    biases = [bias[a], bias[b], bias[3]]
    o, dq, dks, dvs = one_head(qg[0], qg[1], keys, values, biases)
    out[0] = o
    out[1] = dq
    for which, d in ((0, dks), (1, dvs)):
        parts[3, which] = d[2].astype(jnp.bfloat16)
        for w in range(3):
            here = jnp.where(a == w, d[0], jnp.where(b == w, d[1], 0.0))
            parts[w, which] = here.astype(jnp.bfloat16)


def attention(slots, docs_q, docs_k, qg, own, near, mid, far):
    heads = qg.shape[2] // HEAD_DIM
    pair = pl.BlockSpec((2, BLOCK, HEAD_DIM), lambda i, *_: (0, 0, i))
    width = qg.shape[2]
    return pl.pallas_call(
        attend,
        grid_spec=pltpu.PrefetchScalarGridSpec(
            num_scalar_prefetch=1,
            grid=(heads,),
            in_specs=[
                pl.BlockSpec((1, BLOCK), lambda i, *_: (0, 0)),
                pl.BlockSpec((4, BLOCK, 1), lambda i, *_: (0, 0, 0)),
                pair,
                pair,
                pair,
                pair,
                pair,
            ],
            out_specs=[
                pair,
                pl.BlockSpec((4, 2, BLOCK, HEAD_DIM), lambda i, *_: (0, 0, 0, i)),
            ],
            scratch_shapes=[pltpu.VMEM((4, BLOCK, BLOCK), jnp.float32)],
        ),
        out_shape=[
            jax.ShapeDtypeStruct((2, BLOCK, width), jnp.bfloat16),
            jax.ShapeDtypeStruct((4, 2, BLOCK, width), jnp.bfloat16),
        ],
        compiler_params=pltpu.CompilerParams(
            dimension_semantics=("arbitrary",), vmem_limit_bytes=50 * 2**20
        ),
        cost_estimate=pl.CostEstimate(
            flops=heads * 12 * 128 * 512 * 1536 * 3,
            bytes_accessed=20 * BLOCK * width * 2,
            transcendentals=heads * 512 * 1536,
        ),
    )(slots, docs_q, docs_k, qg, own, near, mid, far)


def whole_pass(peers, length, picks, docs, q_ref, k_ref, v_ref, g_ref,
               o_out, dq_out, dk_out, dv_out,
               own, near, mid, far, mate_back, near_back, mid_back, bias,
               in_send, in_recv, in_local, near_send, near_recv, mid_send, mid_recv,
               far_send, far_recv, back_send, mate_back_recv, near_back_recv, mid_back_recv,
               out_send, out_recv, out_local):
    seq = lax.axis_index("seq")
    rank = lax.axis_index("head")
    other = 1 - rank
    heads = own.shape[0]
    rows = q_ref.shape[0]
    width = heads * HEAD_DIM
    parity = lax.rem(seq, 2)
    even = parity == 0
    mate = seq + 1 - 2 * parity
    has_before = seq >= 2
    has_after = seq + 2 < length
    near_to = jnp.where(even, seq + 1, seq + 3)
    near_from = jnp.where(even, seq - 3, seq - 1)
    near_goes = near_to < length
    near_comes = near_from >= 0
    sources = (k_ref, v_ref, q_ref, g_ref)
    results = (dk_out, dv_out, o_out, dq_out)

    def copy(src, dst, send, recv, where):
        return pltpu.make_async_remote_copy(
            src_ref=src, dst_ref=dst, send_sem=send, recv_sem=recv,
            device_id=where, device_id_type=pl.DeviceIdType.MESH,
        )

    def token_rows(r):
        return pl.ds(pl.multiple_of(r * rows, rows), rows)

    def columns(r, g):
        return pl.ds(pl.multiple_of(r * width + g * HEAD_DIM, HEAD_DIM), HEAD_DIM)

    def group(r):
        return pl.ds(pl.multiple_of(r * width, width), width)

    def in_copy(a, g):
        return copy(sources[a].at[:, columns(other, g)], own.at[g, a, token_rows(rank), :],
                    in_send.at[a], in_recv.at[a, g], (seq, other))

    def in_arrival(a, g):
        return copy(sources[a].at[:, columns(other, g)], own.at[g, a, token_rows(other), :],
                    in_send.at[a], in_recv.at[a, g], (seq, other))

    def in_stay(a, g):
        return pltpu.make_async_copy(sources[a].at[:, columns(rank, g)],
                                     own.at[g, a, token_rows(rank), :], in_local.at[a, g])

    def near_copy(g):
        return copy(own.at[g, pl.ds(0, 2)], near.at[g], near_send.at[g], near_recv.at[g],
                    (near_to, rank))

    def mid_copy(g):
        return copy(own.at[g, pl.ds(0, 2)], mid.at[g], mid_send.at[g], mid_recv.at[g],
                    (seq + 2, rank))

    def far_copy(g):
        return copy(mid.at[g], far.at[g], far_send.at[g], far_recv.at[g], (mate, rank))

    def mate_back_copy(g):
        return copy(far.at[g], mate_back.at[g], back_send.at[0], mate_back_recv.at[g],
                    (mate, rank))

    def near_back_copy(g):
        return copy(near.at[g], near_back.at[g], back_send.at[1], near_back_recv.at[g],
                    (near_from, rank))

    def mid_back_copy(g):
        return copy(mid.at[g], mid_back.at[g], back_send.at[2], mid_back_recv.at[g],
                    (seq - 2, rank))

    def out_copy(a, g):
        return copy(own.at[g, a, token_rows(other), :], results[a].at[:, columns(rank, g)],
                    out_send.at[a], out_recv.at[a], (seq, other))

    def out_stay(a, g):
        return pltpu.make_async_copy(own.at[g, a, token_rows(rank), :],
                                     results[a].at[:, columns(rank, g)], out_local.at[a])

    barrier = pltpu.get_barrier_semaphore()

    def greet(where):
        pl.semaphore_signal(barrier, inc=1, device_id=where,
                            device_id_type=pl.DeviceIdType.MESH)

    greet((seq, other))
    greet((mate, rank))

    @pl.when(has_before)
    def _():
        greet((seq - 2, rank))

    @pl.when(has_after)
    def _():
        greet((seq + 2, rank))

    @pl.when(jnp.logical_and(even, near_comes))
    def _():
        greet((near_from, rank))

    @pl.when(jnp.logical_and(jnp.logical_not(even), near_goes))
    def _():
        greet((near_to, rank))

    across = jnp.where(even, near_comes, near_goes)
    pl.semaphore_wait(
        barrier,
        2 + has_before.astype(jnp.int32) + has_after.astype(jnp.int32) + across.astype(jnp.int32),
    )

    def arrive(g):
        for a in range(2):
            in_copy(a, g).start()
            in_stay(a, g).start()

    def follow(g):
        for a in range(2, 4):
            in_copy(a, g).start()
            in_stay(a, g).start()

    for g in range(AHEAD):
        arrive(g)
    follow(0)

    def clear(buffer):
        def one(g, _):
            buffer[g] = jnp.zeros(buffer.shape[1:], buffer.dtype)
            return 0

        lax.fori_loop(0, heads, one, 0)

    @pl.when(jnp.logical_not(has_before))
    def _():
        clear(mid)
        clear(far)

    @pl.when(jnp.logical_not(near_comes))
    def _():
        clear(near)

    @pl.when(jnp.logical_not(near_goes))
    def _():
        clear(near_back)

    @pl.when(jnp.logical_not(has_after))
    def _():
        clear(mid_back)

    offsets = (jnp.where(even, 3, 1), 2, jnp.where(even, 1, 3), 0)
    at_row = lax.broadcasted_iota(jnp.int32, (BLOCK, BLOCK), 0)
    at_col = lax.broadcasted_iota(jnp.int32, (BLOCK, BLOCK), 1)
    for w in range(4):
        block = seq - offsets[w]
        ids = jnp.where(block >= 0, docs[jnp.maximum(block, 0)], -1)
        tall = jnp.broadcast_to(ids.astype(jnp.float32), (HEAD_DIM, BLOCK)).T[:, :1]
        ok = tall == docs[seq].astype(jnp.float32)
        if w == 3:
            ok = jnp.logical_and(ok, at_row <= at_col)
        bias[w] = jnp.where(ok, 0.0, NEGATIVE)

    def slot(pick):
        return jnp.where(pick == 2, 1, jnp.where(pick == offsets[0], 0, 2))

    def spread(g):
        for a in range(2):
            in_arrival(a, g).wait_recv()
            in_stay(a, g).wait()

        @pl.when(has_after)
        def _():
            mid_copy(g).start()

        @pl.when(near_goes)
        def _():
            near_copy(g).start()

    def forward(g):
        @pl.when(has_before)
        def _():
            mid_copy(g).wait_recv()
            far_copy(g).start()

    def compute(g):
        for a in range(2, 4):
            in_arrival(a, g).wait_recv()
            in_stay(a, g).wait()

        @pl.when(near_comes)
        def _():
            near_copy(g).wait_recv()

        @pl.when(has_before)
        def _():
            far_copy(g).wait_recv()
            far_copy(g).wait_send()

        @pl.when(has_after)
        def _():
            mid_copy(g).wait_send()

        @pl.when(near_goes)
        def _():
            near_copy(g).wait_send()

        a, b = slot(picks[0, g, 0]), slot(picks[0, g, 1])

        def pick(n, which):
            return jnp.where(
                n == 0, near[g, which], jnp.where(n == 1, mid[g, which], far[g, which])
            )

        keys = [pick(a, 0), pick(b, 0), own[g, 0]]
        values = [pick(a, 1), pick(b, 1), own[g, 1]]
        biases = [bias[a], bias[b], bias[3]]
        o, dq, dks, dvs = one_head(own[g, 2], own[g, 3], keys, values, biases)
        own[g, 2] = o
        own[g, 3] = dq
        for which, d in ((0, dks), (1, dvs)):
            own[g, which] = d[2].astype(jnp.bfloat16)
            for w, buffer in enumerate((near, mid, far)):
                here = jnp.where(a == w, d[0], jnp.where(b == w, d[1], 0.0))
                buffer[g, which] = here.astype(jnp.bfloat16)

        @pl.when(has_before)
        def _():
            mate_back_copy(g).start()

        @pl.when(near_comes)
        def _():
            near_back_copy(g).start()

        for a in range(2, 4):
            out_copy(a, g).start()
            out_stay(a, g).start()

    def join(g):
        @pl.when(has_before)
        def _():
            mate_back_copy(g).wait_recv()
            both = mid[g].astype(jnp.float32) + mate_back[g].astype(jnp.float32)
            mid[g] = both.astype(jnp.bfloat16)
            mid_back_copy(g).start()

    def finish(g):
        @pl.when(near_goes)
        def _():
            near_back_copy(g).wait_recv()

        @pl.when(has_after)
        def _():
            mid_back_copy(g).wait_recv()

        total = (
            own[g, pl.ds(0, 2)].astype(jnp.float32)
            + near_back[g].astype(jnp.float32)
            + mid_back[g].astype(jnp.float32)
        )
        own[g, pl.ds(0, 2)] = total.astype(jnp.bfloat16)
        for a in range(2):
            out_copy(a, g).start()
            out_stay(a, g).start()

    stages = ((arrive, -AHEAD), (follow, -1), (spread, 0), (forward, LAGS[0]),
              (compute, LAGS[1]), (join, LAGS[2]), (finish, LAGS[3]))

    def step(t, _):
        for stage, lag in stages:
            g = t - lag

            @pl.when(jnp.logical_and(g >= 0, g < heads))
            def _():
                stage(g)

        return 0

    lax.fori_loop(0, heads + LAGS[3], step, 0)

    def drain(view, semaphore):
        pltpu.make_async_copy(view, view, semaphore).wait()

    for a in range(4):
        drain(sources[a].at[:, group(other)], in_send.at[a])
        drain(results[a].at[:, group(rank)], out_send.at[a])
        drain(results[a].at[:, group(rank)], out_local.at[a])
        drain(results[a].at[:, group(other)], out_recv.at[a])

    @pl.when(has_before)
    def _():
        drain(far, back_send.at[0])
        drain(mid, back_send.at[2])

    @pl.when(near_comes)
    def _():
        drain(near, back_send.at[1])


def whole_call(peers, length, picks, docs, queries, key_rows, value_rows, out_grad):
    heads = queries.shape[1] // peers // HEAD_DIM
    window = pltpu.VMEM((heads, 2, BLOCK, HEAD_DIM), jnp.bfloat16)
    dma = pltpu.SemaphoreType.DMA
    hbm = pl.BlockSpec(memory_space=pl.ANY)
    vmem = pl.BlockSpec(memory_space=pltpu.VMEM)
    result = jax.ShapeDtypeStruct(queries.shape, jnp.bfloat16)
    return pl.pallas_call(
        functools.partial(whole_pass, peers, length),
        in_specs=[pl.BlockSpec(memory_space=pltpu.SMEM), vmem, hbm, hbm, hbm, hbm],
        out_specs=[hbm] * 4,
        out_shape=[result] * 4,
        scratch_shapes=[pltpu.VMEM((heads, 4, BLOCK, HEAD_DIM), jnp.bfloat16)]
        + [window] * 6
        + [pltpu.VMEM((4, BLOCK, BLOCK), jnp.float32)]
        + [dma((4,)), dma((4, heads)), dma((4, heads))]
        + [dma((heads,))] * 6
        + [dma((3,))]
        + [dma((heads,))] * 3
        + [dma((4,))] * 3,
        compiler_params=pltpu.CompilerParams(
            collective_id=0, has_side_effects=True, vmem_limit_bytes=60 * 2**20
        ),
        cost_estimate=pl.CostEstimate(
            flops=heads * 12 * 128 * 512 * 1536,
            bytes_accessed=16 * 2**20,
            transcendentals=heads * 512 * 1536,
        ),
    )(picks, docs, queries, key_rows, value_rows, out_grad)


def per_device(queries, key_rows, value_rows, out_grad, doc_ids, picks):
    peers = lax.axis_size("head")
    length = lax.axis_size("seq")
    seq = lax.axis_index("seq")
    rank = lax.axis_index("head")
    rows = queries.shape[0]
    width = queries.shape[1] // peers
    heads = width // HEAD_DIM
    chunks = CHUNKS
    part = width // chunks

    def gather_heads(arrays, c):
        x = jnp.stack(arrays)

        if peers != 2:
            x = x.reshape(2, rows, peers, width)[..., c * part : (c + 1) * part]
            x = lax.all_to_all(x, "head", split_axis=2, concat_axis=1, tiled=True)
            return x.reshape(2, rows * peers, part)

        def columns(r):
            return lax.dynamic_slice_in_dim(x, r * width + c * part, part, 2)

        mine = columns(rank)
        theirs = lax.ppermute(columns(1 - rank), "head", [(0, 1), (1, 0)])
        return jnp.where(
            rank == 0,
            jnp.concatenate([mine, theirs], axis=1),
            jnp.concatenate([theirs, mine], axis=1),
        )

    def give_tokens(x):
        if peers != 2:
            x = lax.all_to_all(x, "head", split_axis=1, concat_axis=2, tiled=True)
            return x.reshape(2, rows, peers, part)

        def tokens(r):
            return lax.dynamic_slice_in_dim(x, r * rows, rows, 1)

        mine = tokens(rank)
        theirs = lax.ppermute(tokens(1 - rank), "head", [(0, 1), (1, 0)])
        return jnp.where(
            rank == 0,
            jnp.stack([mine, theirs], axis=2),
            jnp.stack([theirs, mine], axis=2),
        )

    def inside(pairs):
        return [(a, b) for a, b in pairs if 0 <= a < length and 0 <= b < length]

    two = inside([(s, s + 2) for s in range(length)])
    odd = inside([(s, s + 1 if s % 2 == 0 else s + 3) for s in range(length)])
    mate = inside([(s, s ^ 1) for s in range(length)])

    def back(pairs):
        return [(b, a) for a, b in pairs]

    parity = seq % 2
    local = picks[0].T
    slots = jnp.where(local == 2, 1, jnp.where((local == 1) == (parity == 1), 0, 2))
    offsets = jnp.stack(
        [jnp.where(parity == 1, 1, 3), jnp.int32(2), jnp.where(parity == 1, 3, 1), jnp.int32(0)]
    )
    docs_pad = jnp.concatenate([jnp.full((REACH * BLOCK,), -1, jnp.int32), doc_ids])
    starts = (seq + REACH - offsets) * BLOCK
    docs_k = jnp.stack(
        [lax.dynamic_slice_in_dim(docs_pad, starts[w], BLOCK, 0) for w in range(4)]
    )
    docs_q = docs_k[3:4]
    docs_k = docs_k[:, :, None]

    if peers == 2 and length % 2 == 0:
        return whole_call(
            peers, length, picks, doc_ids.reshape(-1, 1, BLOCK), queries, key_rows, value_rows,
            out_grad,
        )

    per = heads // chunks
    outs, grads = [], []
    for c in range(chunks):
        own = gather_heads([key_rows, value_rows], c)
        qg = gather_heads([queries, out_grad], c)
        near = lax.ppermute(own, "seq", odd)
        mid = lax.ppermute(own, "seq", two)
        far = lax.ppermute(mid, "seq", mate)
        out, parts = attention(
            slots[:, c * per : (c + 1) * per], docs_q, docs_k, qg, own, near, mid, far
        )
        outs.append(give_tokens(out))
        swapped = lax.ppermute(parts[2], "seq", back(mate))
        from_near = lax.ppermute(parts[0], "seq", back(odd))
        joined = (parts[1].astype(jnp.float32) + swapped.astype(jnp.float32)).astype(jnp.bfloat16)
        from_mid = lax.ppermute(joined, "seq", back(two))
        total = (
            parts[3].astype(jnp.float32)
            + from_near.astype(jnp.float32)
            + from_mid.astype(jnp.float32)
        ).astype(jnp.bfloat16)
        grads.append(give_tokens(total))

    def whole(pieces, which):
        x = jnp.stack([p[which] for p in pieces], axis=2)
        return x.reshape(rows, peers * width)

    return (whole(outs, 0), whole(outs, 1), whole(grads, 0), whole(grads, 1))


def solution(mesh):
    tokens = P(("seq", "head"), None)
    return jax.shard_map(
        per_device,
        mesh=mesh,
        in_specs=(tokens, tokens, tokens, tokens, P(), P("seq", "head", None)),
        out_specs=(tokens, tokens, tokens, tokens),
        check_vma=False,
    )
```

```python
import functools
import jax
import jax.numpy as jnp
from jax import lax
from jax.experimental import pallas as pl
from jax.experimental.pallas import tpu as pltpu
from jax.sharding import PartitionSpec as P

HEAD_DIM = 128
BLOCK = 512
REACH = 3
NEGATIVE = -1e30
CHUNKS = 2
AHEAD = 4
LAGS = (2, 4, 5, 8)


def nt(a, b):
    return lax.dot_general(a, b, (((1,), (1,)), ((), ())), preferred_element_type=jnp.float32)


def nn(a, b):
    return lax.dot_general(a, b, (((1,), (0,)), ((), ())), preferred_element_type=jnp.float32)


def one_head(q, g, keys, values, biases):
    scale = HEAD_DIM**-0.5
    scores = [nt(k, q) * scale + b for k, b in zip(keys, biases)]
    top = functools.reduce(
        jnp.maximum, [jnp.max(s, axis=0, keepdims=True) for s in scores]
    )
    exps = [jnp.exp(s - top) for s in scores]
    total = functools.reduce(jnp.add, [jnp.sum(e, axis=0, keepdims=True) for e in exps])
    inverse = 1.0 / total
    probs = [e * inverse for e in exps]
    lows = [p.astype(jnp.bfloat16) for p in probs]
    out_t = functools.reduce(
        jnp.add, [nn(v.T, p) for v, p in zip(values, lows)]
    )
    out_low = out_t.astype(jnp.bfloat16)
    g_t = g.astype(jnp.float32).T
    delta = jnp.sum(out_low.astype(jnp.float32) * g_t, axis=0, keepdims=True)
    grads = [
        (p * (nt(v, g) - delta)).astype(jnp.bfloat16) for p, v in zip(probs, values)
    ]
    dq_t = functools.reduce(jnp.add, [nn(k.T, d) for k, d in zip(keys, grads)]) * scale
    dks = [nn(d, q) * scale for d in grads]
    dvs = [nn(p, g) for p in lows]
    return out_t.T.astype(jnp.bfloat16), dq_t.T.astype(jnp.bfloat16), dks, dvs


def attend(slots, docs_q, docs_k, qg, own, near, mid, far, out, parts, bias):
    i = pl.program_id(0)

    @pl.when(i == 0)
    def _():
        rows = lax.broadcasted_iota(jnp.int32, (BLOCK, BLOCK), 0)
        cols = lax.broadcasted_iota(jnp.int32, (BLOCK, BLOCK), 1)
        for w in range(4):
            ok = docs_k[w] == docs_q[...]
            if w == 3:
                ok = jnp.logical_and(ok, rows <= cols)
            bias[w] = jnp.where(ok, 0.0, NEGATIVE)

    a, b = slots[0, i], slots[1, i]

    def pick(n, which):
        return jnp.where(n == 0, near[which], jnp.where(n == 1, mid[which], far[which]))

    keys = [pick(a, 0), pick(b, 0), own[0]]
    values = [pick(a, 1), pick(b, 1), own[1]]
    biases = [bias[a], bias[b], bias[3]]
    o, dq, dks, dvs = one_head(qg[0], qg[1], keys, values, biases)
    out[0] = o
    out[1] = dq
    for which, d in ((0, dks), (1, dvs)):
        parts[3, which] = d[2].astype(jnp.bfloat16)
        for w in range(3):
            here = jnp.where(a == w, d[0], jnp.where(b == w, d[1], 0.0))
            parts[w, which] = here.astype(jnp.bfloat16)


def attention(slots, docs_q, docs_k, qg, own, near, mid, far):
    heads = qg.shape[2] // HEAD_DIM
    pair = pl.BlockSpec((2, BLOCK, HEAD_DIM), lambda i, *_: (0, 0, i))
    width = qg.shape[2]
    return pl.pallas_call(
        attend,
        grid_spec=pltpu.PrefetchScalarGridSpec(
            num_scalar_prefetch=1,
            grid=(heads,),
            in_specs=[
                pl.BlockSpec((1, BLOCK), lambda i, *_: (0, 0)),
                pl.BlockSpec((4, BLOCK, 1), lambda i, *_: (0, 0, 0)),
                pair,
                pair,
                pair,
                pair,
                pair,
            ],
            out_specs=[
                pair,
                pl.BlockSpec((4, 2, BLOCK, HEAD_DIM), lambda i, *_: (0, 0, 0, i)),
            ],
            scratch_shapes=[pltpu.VMEM((4, BLOCK, BLOCK), jnp.float32)],
        ),
        out_shape=[
            jax.ShapeDtypeStruct((2, BLOCK, width), jnp.bfloat16),
            jax.ShapeDtypeStruct((4, 2, BLOCK, width), jnp.bfloat16),
        ],
        compiler_params=pltpu.CompilerParams(
            dimension_semantics=("arbitrary",), vmem_limit_bytes=50 * 2**20
        ),
        cost_estimate=pl.CostEstimate(
            flops=heads * 12 * 128 * 512 * 1536 * 3,
            bytes_accessed=20 * BLOCK * width * 2,
            transcendentals=heads * 512 * 1536,
        ),
    )(slots, docs_q, docs_k, qg, own, near, mid, far)


def whole_pass(peers, length, picks, docs, q_ref, k_ref, v_ref, g_ref,
               o_out, dq_out, dk_out, dv_out,
               own, near, mid, far, mate_back, near_back, mid_back, bias,
               in_send, in_recv, in_local, near_send, near_recv, mid_send, mid_recv,
               far_send, far_recv, back_send, mate_back_recv, near_back_recv, mid_back_recv,
               out_send, out_recv, out_local):
    seq = lax.axis_index("seq")
    rank = lax.axis_index("head")
    other = 1 - rank
    heads = own.shape[0]
    rows = q_ref.shape[0]
    width = heads * HEAD_DIM
    parity = lax.rem(seq, 2)
    even = parity == 0
    mate = seq + 1 - 2 * parity
    has_before = seq >= 2
    has_after = seq + 2 < length
    near_to = jnp.where(even, seq + 1, seq + 3)
    near_from = jnp.where(even, seq - 3, seq - 1)
    near_goes = near_to < length
    near_comes = near_from >= 0
    sources = (k_ref, v_ref, q_ref, g_ref)
    results = (dk_out, dv_out, o_out, dq_out)

    def copy(src, dst, send, recv, where):
        return pltpu.make_async_remote_copy(
            src_ref=src, dst_ref=dst, send_sem=send, recv_sem=recv,
            device_id=where, device_id_type=pl.DeviceIdType.MESH,
        )

    def token_rows(r):
        return pl.ds(pl.multiple_of(r * rows, rows), rows)

    def columns(r, g):
        return pl.ds(pl.multiple_of(r * width + g * HEAD_DIM, HEAD_DIM), HEAD_DIM)

    def group(r):
        return pl.ds(pl.multiple_of(r * width, width), width)

    def in_copy(a, g):
        return copy(sources[a].at[:, columns(other, g)], own.at[g, a, token_rows(rank), :],
                    in_send.at[a], in_recv.at[a, g], (seq, other))

    def in_arrival(a, g):
        return copy(sources[a].at[:, columns(other, g)], own.at[g, a, token_rows(other), :],
                    in_send.at[a], in_recv.at[a, g], (seq, other))

    def in_stay(a, g):
        return pltpu.make_async_copy(sources[a].at[:, columns(rank, g)],
                                     own.at[g, a, token_rows(rank), :], in_local.at[a, g])

    def near_copy(g):
        return copy(own.at[g, pl.ds(0, 2)], near.at[g], near_send.at[g], near_recv.at[g],
                    (near_to, rank))

    def mid_copy(g):
        return copy(own.at[g, pl.ds(0, 2)], mid.at[g], mid_send.at[g], mid_recv.at[g],
                    (seq + 2, rank))

    def far_copy(g):
        return copy(mid.at[g], far.at[g], far_send.at[g], far_recv.at[g], (mate, rank))

    def mate_back_copy(g):
        return copy(far.at[g], mate_back.at[g], back_send.at[0], mate_back_recv.at[g],
                    (mate, rank))

    def near_back_copy(g):
        return copy(near.at[g], near_back.at[g], back_send.at[1], near_back_recv.at[g],
                    (near_from, rank))

    def mid_back_copy(g):
        return copy(mid.at[g], mid_back.at[g], back_send.at[2], mid_back_recv.at[g],
                    (seq - 2, rank))

    def out_copy(a, g):
        return copy(own.at[g, a, token_rows(other), :], results[a].at[:, columns(rank, g)],
                    out_send.at[a], out_recv.at[a], (seq, other))

    def out_stay(a, g):
        return pltpu.make_async_copy(own.at[g, a, token_rows(rank), :],
                                     results[a].at[:, columns(rank, g)], out_local.at[a])

    barrier = pltpu.get_barrier_semaphore()

    def greet(where):
        pl.semaphore_signal(barrier, inc=1, device_id=where,
                            device_id_type=pl.DeviceIdType.MESH)

    greet((seq, other))
    greet((mate, rank))

    @pl.when(has_before)
    def _():
        greet((seq - 2, rank))

    @pl.when(has_after)
    def _():
        greet((seq + 2, rank))

    @pl.when(jnp.logical_and(even, near_comes))
    def _():
        greet((near_from, rank))

    @pl.when(jnp.logical_and(jnp.logical_not(even), near_goes))
    def _():
        greet((near_to, rank))

    across = jnp.where(even, near_comes, near_goes)
    pl.semaphore_wait(
        barrier,
        2 + has_before.astype(jnp.int32) + has_after.astype(jnp.int32) + across.astype(jnp.int32),
    )

    def arrive(g):
        for a in range(2):
            in_copy(a, g).start()
            in_stay(a, g).start()

    def follow(g):
        for a in range(2, 4):
            in_copy(a, g).start()
            in_stay(a, g).start()

    for g in range(AHEAD):
        arrive(g)
    follow(0)

    def clear(buffer):
        def one(g, _):
            buffer[g] = jnp.zeros(buffer.shape[1:], buffer.dtype)
            return 0

        lax.fori_loop(0, heads, one, 0)

    @pl.when(jnp.logical_not(has_before))
    def _():
        clear(mid)
        clear(far)

    @pl.when(jnp.logical_not(near_comes))
    def _():
        clear(near)

    @pl.when(jnp.logical_not(near_goes))
    def _():
        clear(near_back)

    @pl.when(jnp.logical_not(has_after))
    def _():
        clear(mid_back)

    offsets = (jnp.where(even, 3, 1), 2, jnp.where(even, 1, 3), 0)
    at_row = lax.broadcasted_iota(jnp.int32, (BLOCK, BLOCK), 0)
    at_col = lax.broadcasted_iota(jnp.int32, (BLOCK, BLOCK), 1)
    for w in range(4):
        block = seq - offsets[w]
        ids = jnp.where(block >= 0, docs[jnp.maximum(block, 0)], -1)
        tall = jnp.broadcast_to(ids.astype(jnp.float32), (HEAD_DIM, BLOCK)).T[:, :1]
        ok = tall == docs[seq].astype(jnp.float32)
        if w == 3:
            ok = jnp.logical_and(ok, at_row <= at_col)
        bias[w] = jnp.where(ok, 0.0, NEGATIVE)

    def slot(pick):
        return jnp.where(pick == 2, 1, jnp.where(pick == offsets[0], 0, 2))

    def spread(g):
        for a in range(2):
            in_arrival(a, g).wait_recv()
            in_stay(a, g).wait()

        @pl.when(has_after)
        def _():
            mid_copy(g).start()

        @pl.when(near_goes)
        def _():
            near_copy(g).start()

    def forward(g):
        @pl.when(has_before)
        def _():
            mid_copy(g).wait_recv()
            far_copy(g).start()

    def compute(g):
        for a in range(2, 4):
            in_arrival(a, g).wait_recv()
            in_stay(a, g).wait()

        @pl.when(near_comes)
        def _():
            near_copy(g).wait_recv()

        @pl.when(has_before)
        def _():
            far_copy(g).wait_recv()
            far_copy(g).wait_send()

        @pl.when(has_after)
        def _():
            mid_copy(g).wait_send()

        @pl.when(near_goes)
        def _():
            near_copy(g).wait_send()

        a, b = slot(picks[0, g, 0]), slot(picks[0, g, 1])

        def pick(n, which):
            return jnp.where(
                n == 0, near[g, which], jnp.where(n == 1, mid[g, which], far[g, which])
            )

        keys = [pick(a, 0), pick(b, 0), own[g, 0]]
        values = [pick(a, 1), pick(b, 1), own[g, 1]]
        biases = [bias[a], bias[b], bias[3]]
        o, dq, dks, dvs = one_head(own[g, 2], own[g, 3], keys, values, biases)
        own[g, 2] = o
        own[g, 3] = dq
        for which, d in ((0, dks), (1, dvs)):
            own[g, which] = d[2].astype(jnp.bfloat16)
            for w, buffer in enumerate((near, mid, far)):
                here = jnp.where(a == w, d[0], jnp.where(b == w, d[1], 0.0))
                buffer[g, which] = here.astype(jnp.bfloat16)

        @pl.when(has_before)
        def _():
            mate_back_copy(g).start()

        for a in range(2, 4):
            out_copy(a, g).start()
            out_stay(a, g).start()

    def join(g):
        @pl.when(has_before)
        def _():
            mate_back_copy(g).wait_recv()
            both = mid[g].astype(jnp.float32) + mate_back[g].astype(jnp.float32)
            mid[g] = both.astype(jnp.bfloat16)
            mid_back_copy(g).start()

        @pl.when(near_comes)
        def _():
            near_back_copy(g).start()

    def finish(g):
        @pl.when(near_goes)
        def _():
            near_back_copy(g).wait_recv()

        @pl.when(has_after)
        def _():
            mid_back_copy(g).wait_recv()

        total = (
            own[g, pl.ds(0, 2)].astype(jnp.float32)
            + near_back[g].astype(jnp.float32)
            + mid_back[g].astype(jnp.float32)
        )
        own[g, pl.ds(0, 2)] = total.astype(jnp.bfloat16)
        for a in range(2):
            out_copy(a, g).start()
            out_stay(a, g).start()

    stages = ((arrive, -AHEAD), (follow, -1), (spread, 0), (forward, LAGS[0]),
              (compute, LAGS[1]), (join, LAGS[2]), (finish, LAGS[3]))

    def step(t, _):
        for stage, lag in stages:
            g = t - lag

            @pl.when(jnp.logical_and(g >= 0, g < heads))
            def _():
                stage(g)

        return 0

    lax.fori_loop(0, heads + LAGS[3], step, 0)

    def drain(view, semaphore):
        pltpu.make_async_copy(view, view, semaphore).wait()

    for a in range(4):
        drain(sources[a].at[:, group(other)], in_send.at[a])
        drain(results[a].at[:, group(rank)], out_send.at[a])
        drain(results[a].at[:, group(rank)], out_local.at[a])
        drain(results[a].at[:, group(other)], out_recv.at[a])

    @pl.when(has_before)
    def _():
        drain(far, back_send.at[0])
        drain(mid, back_send.at[2])

    @pl.when(near_comes)
    def _():
        drain(near, back_send.at[1])


def whole_call(peers, length, picks, docs, queries, key_rows, value_rows, out_grad):
    heads = queries.shape[1] // peers // HEAD_DIM
    window = pltpu.VMEM((heads, 2, BLOCK, HEAD_DIM), jnp.bfloat16)
    dma = pltpu.SemaphoreType.DMA
    hbm = pl.BlockSpec(memory_space=pl.ANY)
    vmem = pl.BlockSpec(memory_space=pltpu.VMEM)
    result = jax.ShapeDtypeStruct(queries.shape, jnp.bfloat16)
    return pl.pallas_call(
        functools.partial(whole_pass, peers, length),
        in_specs=[pl.BlockSpec(memory_space=pltpu.SMEM), vmem, hbm, hbm, hbm, hbm],
        out_specs=[hbm] * 4,
        out_shape=[result] * 4,
        scratch_shapes=[pltpu.VMEM((heads, 4, BLOCK, HEAD_DIM), jnp.bfloat16)]
        + [window] * 6
        + [pltpu.VMEM((4, BLOCK, BLOCK), jnp.float32)]
        + [dma((4,)), dma((4, heads)), dma((4, heads))]
        + [dma((heads,))] * 6
        + [dma((3,))]
        + [dma((heads,))] * 3
        + [dma((4,))] * 3,
        compiler_params=pltpu.CompilerParams(
            collective_id=0, has_side_effects=True, vmem_limit_bytes=60 * 2**20
        ),
        cost_estimate=pl.CostEstimate(
            flops=heads * 12 * 128 * 512 * 1536,
            bytes_accessed=16 * 2**20,
            transcendentals=heads * 512 * 1536,
        ),
    )(picks, docs, queries, key_rows, value_rows, out_grad)


def per_device(queries, key_rows, value_rows, out_grad, doc_ids, picks):
    peers = lax.axis_size("head")
    length = lax.axis_size("seq")
    seq = lax.axis_index("seq")
    rank = lax.axis_index("head")
    rows = queries.shape[0]
    width = queries.shape[1] // peers
    heads = width // HEAD_DIM
    chunks = CHUNKS
    part = width // chunks

    def gather_heads(arrays, c):
        x = jnp.stack(arrays)

        if peers != 2:
            x = x.reshape(2, rows, peers, width)[..., c * part : (c + 1) * part]
            x = lax.all_to_all(x, "head", split_axis=2, concat_axis=1, tiled=True)
            return x.reshape(2, rows * peers, part)

        def columns(r):
            return lax.dynamic_slice_in_dim(x, r * width + c * part, part, 2)

        mine = columns(rank)
        theirs = lax.ppermute(columns(1 - rank), "head", [(0, 1), (1, 0)])
        return jnp.where(
            rank == 0,
            jnp.concatenate([mine, theirs], axis=1),
            jnp.concatenate([theirs, mine], axis=1),
        )

    def give_tokens(x):
        if peers != 2:
            x = lax.all_to_all(x, "head", split_axis=1, concat_axis=2, tiled=True)
            return x.reshape(2, rows, peers, part)

        def tokens(r):
            return lax.dynamic_slice_in_dim(x, r * rows, rows, 1)

        mine = tokens(rank)
        theirs = lax.ppermute(tokens(1 - rank), "head", [(0, 1), (1, 0)])
        return jnp.where(
            rank == 0,
            jnp.stack([mine, theirs], axis=2),
            jnp.stack([theirs, mine], axis=2),
        )

    def inside(pairs):
        return [(a, b) for a, b in pairs if 0 <= a < length and 0 <= b < length]

    two = inside([(s, s + 2) for s in range(length)])
    odd = inside([(s, s + 1 if s % 2 == 0 else s + 3) for s in range(length)])
    mate = inside([(s, s ^ 1) for s in range(length)])

    def back(pairs):
        return [(b, a) for a, b in pairs]

    parity = seq % 2
    local = picks[0].T
    slots = jnp.where(local == 2, 1, jnp.where((local == 1) == (parity == 1), 0, 2))
    offsets = jnp.stack(
        [jnp.where(parity == 1, 1, 3), jnp.int32(2), jnp.where(parity == 1, 3, 1), jnp.int32(0)]
    )
    docs_pad = jnp.concatenate([jnp.full((REACH * BLOCK,), -1, jnp.int32), doc_ids])
    starts = (seq + REACH - offsets) * BLOCK
    docs_k = jnp.stack(
        [lax.dynamic_slice_in_dim(docs_pad, starts[w], BLOCK, 0) for w in range(4)]
    )
    docs_q = docs_k[3:4]
    docs_k = docs_k[:, :, None]

    if peers == 2 and length % 2 == 0:
        return whole_call(
            peers, length, picks, doc_ids.reshape(-1, 1, BLOCK), queries, key_rows, value_rows,
            out_grad,
        )

    per = heads // chunks
    outs, grads = [], []
    for c in range(chunks):
        own = gather_heads([key_rows, value_rows], c)
        qg = gather_heads([queries, out_grad], c)
        near = lax.ppermute(own, "seq", odd)
        mid = lax.ppermute(own, "seq", two)
        far = lax.ppermute(mid, "seq", mate)
        out, parts = attention(
            slots[:, c * per : (c + 1) * per], docs_q, docs_k, qg, own, near, mid, far
        )
        outs.append(give_tokens(out))
        swapped = lax.ppermute(parts[2], "seq", back(mate))
        from_near = lax.ppermute(parts[0], "seq", back(odd))
        joined = (parts[1].astype(jnp.float32) + swapped.astype(jnp.float32)).astype(jnp.bfloat16)
        from_mid = lax.ppermute(joined, "seq", back(two))
        total = (
            parts[3].astype(jnp.float32)
            + from_near.astype(jnp.float32)
            + from_mid.astype(jnp.float32)
        ).astype(jnp.bfloat16)
        grads.append(give_tokens(total))

    def whole(pieces, which):
        x = jnp.stack([p[which] for p in pieces], axis=2)
        return x.reshape(rows, peers * width)

    return (whole(outs, 0), whole(outs, 1), whole(grads, 0), whole(grads, 1))


def solution(mesh):
    tokens = P(("seq", "head"), None)
    return jax.shard_map(
        per_device,
        mesh=mesh,
        in_specs=(tokens, tokens, tokens, tokens, P(), P("seq", "head", None)),
        out_specs=(tokens, tokens, tokens, tokens),
        check_vma=False,
    )
```
